256 devices in a mesh: tm: 32 (over y, z_lo, core), space: 8 (over x, z_hi).
Axes of the slice: x: 4, y: 4, z: 8 (z_hi: 2, z_lo: 4; z = z_hi * 4 + z_lo), core: 2. Of those that a mesh axis runs over, the one named last changes fastest.
Arguments:
- nodes: float32 [32, 3, 32, 128, 256], P('tm', None, 'space'), may hold values from -6 to 6
- coefficients: bfloat16 [7, 32, 128, 256], P(None, 'space'), may hold values from -0.3 to 1, as said below
Outputs:
- new_nodes: float32 [32, 3, 32, 128, 256], P('tm', None, 'space')
The draws below stay inside these ranges and needn't reach their ends.
Inputs may be any that keep to these rules, and one draw needn't show every extreme that they name: `coefficients`: entries 0 to 2 lie in [0.25, 1]; entry 3 is at most 0.3 sqrt(K0 K1) in magnitude, entry 4 0.3 sqrt(K0 K2), entry 5 0.3 sqrt(K1 K2); the rate lies in [0.02, 0.5].
All inputs are finite; a program needn't handle non-finite values.
Results may differ from the reference program's by a relative error of at most 0.0003.
Values sent between devices are 32-bit elements; how exact they have to be, the bound alone decides.
A program may use at most 64 MiB of HBM per device.

```python
import math
import jax
import jax.numpy as jnp
from jax import lax

NX = 128
NY = 256
NODES = 3
NT = 32
NZ = 32


def draw_coefficients(key, part):
    key = jax.random.fold_in(key, 11)
    key_diag, key_off, key_rate = jax.random.split(key, 3)
    diagonal = jnp.exp(jax.random.uniform(key_diag, (3, NZ, NX, NY), jnp.float32, math.log(0.25), 0.0))
    rate = jnp.exp(jax.random.uniform(key_rate, (1, NZ, NX, NY), jnp.float32, math.log(0.02), math.log(0.5)))
    spread = jax.random.uniform(key_off, (3, NZ, NX, NY), jnp.float32, -0.3, 0.3)
    roots = jnp.sqrt(diagonal)
    scales = jnp.stack([roots[0] * roots[1], roots[0] * roots[2], roots[1] * roots[2]])
    return jnp.concatenate([diagonal, spread * scales, rate], axis=0).astype(jnp.bfloat16)


def block_levels(rng, shape, pieces, least, high):
    def one(axis_at, parts):
        heights = jax.random.uniform(jax.random.fold_in(jax.random.fold_in(rng, 6), axis_at), (parts,), jnp.float32, least / len(pieces), high / len(pieces))
        return jnp.repeat(jnp.exp(heights), shape[axis_at] // parts).reshape((-1,) + (1,) * (len(shape) - axis_at - 1))

    loudness = one(*pieces[0])
    for cut in pieces[1:]:
        loudness = loudness * one(*cut)
    return loudness


def bell_draw(key, extent, scale, limit, shards=(), dtype=jnp.bfloat16):
    values = jax.random.normal(key, extent, jnp.float32) * scale
    if len(shards) > 0:
        values = block_levels(key, extent, shards, -0.22, 0.18) * values
    return jnp.clip(values, min=-limit, max=limit).astype(dtype)


def setup_inputs(seed: int = 0) -> dict:
    key_list = jax.random.split(jax.random.key(seed), 3)
    return {
        "nodes": bell_draw(key_list[0], (NT, NODES, NZ, NX, NY), 1.0, 6.0, ((0, 32), (2, 8)), jnp.float32),
        "coefficients": draw_coefficients(jax.random.fold_in(key_list[2], 71), 0),
    }


step_length = 0.2
node_step = 0.1
weight_a0 = 0.2 * 5.0 / 24.0
weight_a1 = 0.2 / 3.0
weight_a2 = -0.2 / 24.0
weight_b0 = -0.2 / 24.0
weight_b1 = 0.2 / 3.0
weight_b2 = 0.2 * 5.0 / 24.0


def operate(padded, coeffs, spacing):
    full = jnp.pad(padded, ((0, 0), (0, 0), (1, 1), (1, 1)))
    centre = full[:, 1:-1, 1:-1, 1:-1]
    second_z = full[:, 2:, 1:-1, 1:-1] - 2.0 * centre + full[:, :-2, 1:-1, 1:-1]
    second_x = (full[:, 1:-1, 2:, 1:-1] - 2.0 * centre + full[:, 1:-1, :-2, 1:-1]) / (spacing * spacing)
    second_y = (full[:, 1:-1, 1:-1, 2:] - 2.0 * centre + full[:, 1:-1, 1:-1, :-2]) / (spacing * spacing)
    cross_zx = (full[:, 2:, 2:, 1:-1] - full[:, 2:, :-2, 1:-1] - full[:, :-2, 2:, 1:-1] + full[:, :-2, :-2, 1:-1]) / (2.0 * spacing)
    cross_zy = (full[:, 2:, 1:-1, 2:] - full[:, 2:, 1:-1, :-2] - full[:, :-2, 1:-1, 2:] + full[:, :-2, 1:-1, :-2]) / (2.0 * spacing)
    cross_xy = (full[:, 1:-1, 2:, 2:] - full[:, 1:-1, 2:, :-2] - full[:, 1:-1, :-2, 2:] + full[:, 1:-1, :-2, :-2]) / (2.0 * spacing * spacing)
    total = coeffs[0] * second_z + coeffs[1] * second_x + coeffs[2] * second_y
    total = total + coeffs[3] * cross_zx + coeffs[4] * cross_zy + coeffs[5] * cross_xy
    return total - coeffs[6] * centre


def restrict(field):
    summed = field[..., 0::2, 0::2] + field[..., 0::2, 1::2] + field[..., 1::2, 0::2] + field[..., 1::2, 1::2]
    return summed * 0.25


def prolong(field):
    return jnp.repeat(jnp.repeat(field, 2, axis=-2), 2, axis=-1)


def zero_rim(field):
    return jnp.pad(field, ((0, 0), (1, 1), (0, 0), (0, 0)))


def fine_slice(values, coeffs, coarse):
    forces = operate(zero_rim(values), coeffs, 1.0)
    first = values[0] + (weight_a0 * forces[0] + weight_a1 * forces[1] + weight_a2 * forces[2])
    first_force = operate(zero_rim(first[None]), coeffs, 1.0)[0]
    last = first + node_step * (first_force - forces[1]) + (weight_b0 * forces[0] + weight_b1 * forces[1] + weight_b2 * forces[2])
    last_force = operate(zero_rim(last[None]), coeffs, 1.0)[0]
    simpson = step_length * (forces[0] / 6.0 + first_force * (2.0 / 3.0) + last_force / 6.0)
    start_coarse = restrict(values[0])
    start_force = operate(zero_rim(start_coarse[None]), coarse, 2.0)[0]
    constant = restrict(simpson) - step_length * start_force
    return first, last, start_coarse, restrict(last), constant


def reference(nodes, coefficients):
    coeffs = coefficients.astype(jnp.float32)
    coarse = restrict(coeffs)
    first, last, start_coarse, end_coarse, constant = lax.map(lambda values: fine_slice(values, coeffs, coarse), nodes)

    def link(start, constant_here):
        end = start + step_length * operate(zero_rim(start[None]), coarse, 2.0)[0] + constant_here
        return end, (start, end)

    unused, (starts, ends) = lax.scan(link, start_coarse[0], constant)
    middle = first + prolong(((starts - start_coarse) + (ends - end_coarse)) * 0.5)
    final = last + prolong(ends - end_coarse)
    head = jnp.concatenate([nodes[0:1, 0], final[:-1]], axis=0)
    return jnp.stack([head, middle, final], axis=1)
```

```python
import functools

import jax
import jax.numpy as jnp
from jax import lax
from jax.experimental import pallas as pl
from jax.experimental.pallas import tpu as pltpu
from jax.sharding import PartitionSpec as P

MESH = pl.DeviceIdType.MESH
F32 = jnp.float32
HIGH = lax.Precision.HIGHEST

A0, A1, A2 = 0.2 * 5.0 / 24.0, 0.2 / 3.0, -0.2 / 24.0
B0, B1, B2 = -0.2 / 24.0, 0.2 / 3.0, 0.2 * 5.0 / 24.0
C0, C1 = 0.2 / 6.0, 0.2 * 2.0 / 3.0

DEPTH = 4
ROWS, COLS = 128, 256
HALF, LANES = 64, 128
SLABS = 8
BLOCK = 8
NT = 32
RIM = 8
STRIP = 32
WIN = 24


def worker_place(j):
    return 6 - 6 * lax.rem(j, 2)


def neighbours(value, axis, size, mask_low, mask_high):
    ahead = pltpu.roll(value, size - 1, axis)
    behind = pltpu.roll(value, 1, axis)
    return jnp.where(mask_high, 0.0, ahead), jnp.where(mask_low, 0.0, behind)


def rows_around(value, size):
    return pltpu.roll(value, size - 1, 0), pltpu.roll(value, 1, 0)


def stencil(low, here, high, k, height, width, top, rows):
    lane = lax.broadcasted_iota(jnp.int32, (height, width), 1)
    first, last = lane == 0, lane == width - 1
    cut = lambda v: v[top : top + rows]
    over_z = high - low
    right, left = neighbours(here, 1, width, first, last)
    slope = right - left
    d_right, d_left = neighbours(over_z, 1, width, first, last)
    down, up = rows_around(here, height)
    z_down, z_up = rows_around(over_z, height)
    s_down, s_up = rows_around(slope, height)
    total = k[0] * cut(high + low) + k[1] * cut(down + up) + k[2] * cut(right + left)
    total = total + k[3] * cut(z_down - z_up) + k[4] * cut(d_right - d_left)
    total = total + k[5] * cut(s_down - s_up)
    return total + k[6] * cut(here)


def pair_matrix(shape, long_axis, value):
    long = lax.broadcasted_iota(jnp.int32, shape, long_axis)
    short = lax.broadcasted_iota(jnp.int32, shape, 1 - long_axis)
    return jnp.where((long == 2 * short) | (long == 2 * short + 1), value, 0.0).astype(F32)


def restrict(plane):
    across = jnp.dot(plane, pair_matrix((COLS, LANES), 0, 0.5), precision=HIGH, preferred_element_type=F32)
    return jnp.dot(pair_matrix((HALF, ROWS), 1, 0.5), across, precision=HIGH, preferred_element_type=F32)


def prolong(plane):
    along = jnp.dot(pair_matrix((ROWS, HALF), 0, 1.0), plane, precision=HIGH, preferred_element_type=F32)
    return jnp.dot(along, pair_matrix((LANES, COLS), 1, 1.0), precision=HIGH, preferred_element_type=F32)


def loop(count, fn, unroll=1):
    def step(i, carry):
        fn(i)
        return carry

    lax.fori_loop(0, count, step, 0, unroll=unroll)


def kernel(
    nodes, coeffs, out,
    kf, ab, bb, cb, v1, v2, v2p, kcp, rp, w0, wn, kb, rb, hb, ec, en,
    halo_s, halo_r, shift_s, shift_r, k_s, k_r, r_s, r_r, hand_s, hand_r, e_s, e_r, f_s, f_r, known,
):
    t = lax.axis_index("tm")
    s = lax.axis_index("space")
    block = lax.div(t, BLOCK)
    place = lax.rem(t, BLOCK)
    base = block * BLOCK
    is_worker = place == worker_place(s)
    strips = ROWS // STRIP

    def tell(sem, tm, sp):
        pl.semaphore_signal(sem, inc=1, device_id=(tm, sp), device_id_type=MESH)

    barrier = pltpu.get_barrier_semaphore()
    for n in range(1, SLABS):
        tell(barrier, t, lax.rem(s + n, SLABS))
    for n in range(1, BLOCK):
        tell(barrier, base + lax.rem(place + n, BLOCK), s)

    cross_up = (place == BLOCK - 1) & (t < NT - 1)
    cross_down = (place == 0) & (t > 0)

    @pl.when(cross_up)
    def _():
        tell(barrier, t + 1, s)

    @pl.when(cross_down)
    def _():
        tell(barrier, t - 1, s)

    for dj in (-1, 0, 1):
        j = s + dj

        @pl.when(is_worker & (block > 0) & (j >= 0) & (j < SLABS))
        def _(j=j):
            tell(barrier, base - BLOCK + worker_place(j), j)

    for buf in (ab, bb, cb):
        buf[:, 0:RIM, :] = jnp.zeros((DEPTH + 2, RIM, COLS), F32)
        buf[:, RIM + ROWS :, :] = jnp.zeros((DEPTH + 2, RIM, COLS), F32)

    @pl.when(s == 0)
    def _():
        for buf in (ab, bb, cb):
            buf[0, RIM : RIM + ROWS, :] = jnp.zeros((ROWS, COLS), F32)

    @pl.when(s == SLABS - 1)
    def _():
        for buf in (ab, bb, cb):
            buf[DEPTH + 1, RIM : RIM + ROWS, :] = jnp.zeros((ROWS, COLS), F32)

    kcp[:, :, 0:RIM, :] = jnp.zeros((7, DEPTH, RIM, LANES), F32)
    kcp[:, :, RIM + HALF :, :] = jnp.zeros((7, DEPTH, RIM, LANES), F32)
    rp[:, 0:RIM, :] = jnp.zeros((DEPTH, RIM, LANES), F32)
    rp[:, RIM + HALF :, :] = jnp.zeros((DEPTH, RIM, LANES), F32)

    def combine_a(p, i):
        here = pl.ds(pl.multiple_of(i * STRIP, STRIP), STRIP)
        there = pl.ds(pl.multiple_of(RIM + i * STRIP, 8), STRIP)
        ab[p + 1, there, :] = A0 * nodes[0, 0, p, here, :] + A1 * nodes[0, 1, p, here, :] + A2 * nodes[0, 2, p, here, :]

    loop(strips, lambda i: combine_a(0, i))
    loop(strips, lambda i: combine_a(3, i))

    expect = 14 + jnp.where(cross_up, 1, 0) + jnp.where(cross_down, 1, 0)
    hands = 3 - jnp.where(s == 0, 1, 0) - jnp.where(s == SLABS - 1, 1, 0)
    expect = expect + jnp.where(is_worker & (block < NT // BLOCK - 1), hands, 0)
    pl.semaphore_wait(barrier, expect)

    inner = pl.ds(RIM, ROWS)

    def halo(buf, phase, upward):
        return pltpu.make_async_remote_copy(
            src_ref=buf.at[DEPTH if upward else 1, inner],
            dst_ref=buf.at[0 if upward else DEPTH + 1, inner],
            send_sem=halo_s.at[phase, int(upward)],
            recv_sem=halo_r.at[phase, int(upward)],
            device_id=(t, s + 1 if upward else s - 1),
            device_id_type=MESH,
        )

    def send_halo(buf, phase, upward):
        @pl.when(s < SLABS - 1 if upward else s > 0)
        def _():
            halo(buf, phase, upward).start()

    def take_halo(buf, phase, upward):
        @pl.when(s > 0 if upward else s < SLABS - 1)
        def _():
            halo(buf, phase, upward).wait_recv()

    send_halo(ab, 0, False)
    send_halo(ab, 0, True)
    for n in range(1, BLOCK):
        tell(known, base + lax.rem(place + n, BLOCK), s)

    def shift(src, dst, n, tm):
        return pltpu.make_async_remote_copy(
            src_ref=src, dst_ref=dst, send_sem=shift_s.at[n], recv_sem=shift_r.at[n],
            device_id=(tm, s), device_id_type=MESH,
        )

    send_w0 = shift(w0, wn, 0, t - 1)
    send_v2 = shift(v2, v2p, 1, t + 1)

    def start_coarse(p):
        w0[p] = restrict(nodes[0, 0, p])

    loop(DEPTH, start_coarse)

    @pl.when(t > 0)
    def _():
        send_w0.start()

    @pl.when(t == NT - 1)
    def _():
        wn[...] = jnp.zeros_like(wn)

    def weights(p, i):
        here = pl.ds(pl.multiple_of(i * STRIP, STRIP), STRIP)
        k = [coeffs[m, p, here, :].astype(F32) for m in range(7)]
        for m in range(3):
            kf[m, p, here, :] = k[m]
            kf[3 + m, p, here, :] = 0.5 * k[3 + m]
        kf[6, p, here, :] = -(2.0 * (k[0] + k[1] + k[2]) + k[6])

    loop(DEPTH * strips, lambda n: weights(lax.div(n, strips), lax.rem(n, strips)))
    loop(strips, lambda i: combine_a(1, i))
    loop(strips, lambda i: combine_a(2, i))

    def force(buf, p, i):
        window = pl.ds(pl.multiple_of(i * STRIP, STRIP), STRIP + 2 * RIM)
        here = pl.ds(pl.multiple_of(i * STRIP, STRIP), STRIP)
        return stencil(
            buf[p, window, :], buf[p + 1, window, :], buf[p + 2, window, :],
            [kf[m, p, here, :] for m in range(7)], STRIP + 2 * RIM, COLS, RIM, STRIP,
        )

    def spots(i):
        return (
            pl.ds(pl.multiple_of(i * STRIP, STRIP), STRIP),
            pl.ds(pl.multiple_of(RIM + i * STRIP, 8), STRIP),
        )

    def first_node(p, i):
        here, there = spots(i)
        value = nodes[0, 0, p, here, :] + force(ab, p, i)
        v1[p, here, :] = value
        bb[p + 1, there, :] = (
            0.1 * value + B0 * nodes[0, 0, p, here, :] + (B1 - 0.1) * nodes[0, 1, p, here, :] + B2 * nodes[0, 2, p, here, :]
        )

    def last_node(p, i):
        here, there = spots(i)
        first = v1[p, here, :]
        value = first + force(bb, p, i)
        v2[p, here, :] = value
        cb[p + 1, there, :] = C0 * (nodes[0, 0, p, here, :] + value) + C1 * first

    def add_force(p, i):
        here, there = spots(i)
        out[0, 0, p, here, :] = nodes[0, 0, p, here, :] + force(cb, p, i)

    def planes(fn, which):
        for p in which:
            loop(strips, lambda i, p=p: fn(p, i))

    def coarse_weights(n):
        m, p = lax.div(n, DEPTH), lax.rem(n, DEPTH)
        plane = coeffs[m, p].astype(F32)
        kcp[m, p, RIM : RIM + HALF, :] = restrict(plane)

    loop(7 * DEPTH, coarse_weights)

    def scale_weights(p):
        here = slice(RIM, RIM + HALF)
        k = [kcp[m, p, here, :] for m in range(7)]
        kcp[0, p, here, :] = 0.2 * k[0]
        for m in range(1, 5):
            kcp[m, p, here, :] = 0.05 * k[m]
        kcp[5, p, here, :] = 0.025 * k[5]
        kcp[6, p, here, :] = 1.0 - (0.4 * k[0] + 0.1 * (k[1] + k[2]) + 0.2 * k[6])

    loop(DEPTH, scale_weights)
    planes(first_node, (1, 2))
    pl.semaphore_wait(known, BLOCK - 1)

    goal = worker_place(place)
    k_self = (goal == place) & (place == s)
    window = pl.ds(pl.multiple_of(8 * place, 8), WIN)
    slab = pl.ds(pl.multiple_of(DEPTH * s, DEPTH), DEPTH)
    send_k = pltpu.make_async_remote_copy(
        src_ref=kcp.at[:, :, window], dst_ref=kb.at[:, slab], send_sem=k_s.at[0], recv_sem=k_r.at[0],
        device_id=(base + goal, place), device_id_type=MESH,
    )

    @pl.when(k_self)
    def _():
        pltpu.make_async_copy(kcp.at[:, :, window], kb.at[:, slab], k_r.at[0]).start()

    @pl.when(jnp.logical_not(k_self))
    def _():
        send_k.start()

    take_halo(ab, 0, True)
    planes(first_node, (0,))
    send_halo(bb, 1, False)
    take_halo(ab, 0, False)
    planes(first_node, (3,))
    send_halo(bb, 1, True)
    planes(last_node, (1, 2))
    take_halo(bb, 1, True)
    planes(last_node, (0,))
    send_halo(cb, 2, False)
    take_halo(bb, 1, False)
    planes(last_node, (3,))
    send_halo(cb, 2, True)

    @pl.when(t < NT - 1)
    def _():
        send_v2.start()

    planes(add_force, (1, 2))
    take_halo(cb, 2, True)
    planes(add_force, (0,))
    take_halo(cb, 2, False)
    planes(add_force, (3,))

    @pl.when(t < NT - 1)
    def _():
        send_w0.wait_recv()

    def right_side(p):
        rp[p, RIM : RIM + HALF, :] = restrict(out[0, 0, p]) - wn[p]

    loop(DEPTH, right_side)

    def send_r(j):
        to = worker_place(j)
        rows = pl.ds(pl.multiple_of(8 * j, 8), WIN)
        own = (to == place) & (j == s)
        copy = pltpu.make_async_remote_copy(
            src_ref=rp.at[:, rows], dst_ref=rb.at[place, slab], send_sem=r_s.at[j], recv_sem=r_r.at[place],
            device_id=(base + to, j), device_id_type=MESH,
        )
        return own, copy, pltpu.make_async_copy(rp.at[:, rows], rb.at[place, slab], r_r.at[place])

    def start_r(j):
        own, copy, local = send_r(j)

        @pl.when(own)
        def _():
            local.start()

        @pl.when(jnp.logical_not(own))
        def _():
            copy.start()

    loop(SLABS, start_r)

    @pl.when(t > 0)
    def _():
        send_v2.wait_recv()

    def early(p):
        @pl.when(t > 0)
        def _():
            out[0, 0, p] = v2p[p] + prolong(restrict(nodes[0, 0, p] - v2p[p]))

        @pl.when(t == 0)
        def _():
            out[0, 0, p] = nodes[0, 0, p]

        gap = prolong(wn[p] - restrict(v2[p]))
        out[0, 1, p] = v1[p] + 0.5 * gap
        out[0, 2, p] = v2[p] + gap

    loop(DEPTH, early)

    def hand(dj):
        j = s + dj
        return pltpu.make_async_remote_copy(
            src_ref=hb.at[BLOCK, pl.ds(1, 32), pl.ds(8, 8)],
            dst_ref=hb.at[0, pl.ds(1, 32), pl.ds(8 - 8 * dj, 8)],
            send_sem=hand_s.at[dj + 1],
            recv_sem=hand_r.at[dj + 1],
            device_id=(base + BLOCK + worker_place(j), j),
            device_id_type=MESH,
        )

    def spread(h, to):
        src = hb.at[h + 1, pl.ds(1 + DEPTH * to, DEPTH), pl.ds(8, 8)]
        dst = en.at[:, pl.ds(pl.multiple_of(8 * s, 8), 8)]
        own = (h == place) & (to == s)
        copy = pltpu.make_async_remote_copy(
            src_ref=src, dst_ref=dst, send_sem=e_s.at[h, to], recv_sem=e_r.at[0],
            device_id=(base + h, to), device_id_type=MESH,
        )
        return own, copy, pltpu.make_async_copy(src, dst, e_r.at[0])

    def start_spread(h):
        def one(to):
            own, copy, local = spread(h, to)

            @pl.when(own)
            def _():
                local.start()

            @pl.when(jnp.logical_not(own))
            def _():
                copy.start()

        loop(SLABS, one)

    @pl.when(is_worker)
    def _():
        def clear(h):
            hb[h, 0] = jnp.zeros((WIN, LANES), F32)
            hb[h, 33] = jnp.zeros((WIN, LANES), F32)

        loop(BLOCK + 1, clear)

        @pl.when(block == 0)
        def _():
            hb[0, 1:33] = jnp.zeros((32, WIN, LANES), F32)

        @pl.when((block > 0) & (s == 0))
        def _():
            hb[0, 1:33, 0:8, :] = jnp.zeros((32, 8, LANES), F32)

        @pl.when((block > 0) & (s == SLABS - 1))
        def _():
            hb[0, 1:33, 16:24, :] = jnp.zeros((32, 8, LANES), F32)

        pltpu.make_async_copy(kb, kb, k_r.at[0]).wait()
        for dj in (-1, 0, 1):
            @pl.when((block > 0) & (s - dj >= 0) & (s - dj < SLABS))
            def _(dj=dj):
                hand(dj).wait_recv()

        def advance(h):
            pltpu.make_async_copy(rb.at[h], rb.at[h], r_r.at[h]).wait()

            def plane(p):
                value = stencil(
                    hb[h, p], hb[h, p + 1], hb[h, p + 2],
                    [kb[m, p] for m in range(7)], WIN, LANES, 0, WIN,
                )
                hb[h + 1, p + 1] = value + rb[h, p]

            loop(32, plane, unroll=2)

            @pl.when(block == NT // BLOCK - 1)
            def _():
                start_spread(h)

        loop(BLOCK, advance)

        @pl.when(block < NT // BLOCK - 1)
        def _():
            for dj in (-1, 0, 1):
                j = s + dj

                @pl.when((j >= 0) & (j < SLABS))
                def _(dj=dj):
                    hand(dj).start()

            loop(BLOCK, start_spread)

    pltpu.make_async_copy(en, en, e_r.at[0]).wait()
    forward = pltpu.make_async_remote_copy(
        src_ref=en, dst_ref=ec, send_sem=f_s.at[0], recv_sem=f_r.at[0], device_id=(t + 1, s), device_id_type=MESH
    )

    @pl.when(t < NT - 1)
    def _():
        forward.start()

    def end_node(p):
        gain = prolong(en[p])
        out[0, 2, p] += gain
        out[0, 1, p] += 0.5 * gain

    loop(DEPTH, end_node)

    @pl.when(t > 0)
    def _():
        forward.wait_recv()

        def start_node(p):
            gain = prolong(ec[p])
            out[0, 0, p] += gain
            out[0, 1, p] += 0.5 * gain

        loop(DEPTH, start_node)

    for phase, buf in enumerate((ab, bb, cb)):

        @pl.when(s < SLABS - 1)
        def _(phase=phase, buf=buf):
            halo(buf, phase, True).wait_send()

        @pl.when(s > 0)
        def _(phase=phase, buf=buf):
            halo(buf, phase, False).wait_send()

    @pl.when(t > 0)
    def _():
        send_w0.wait_send()

    @pl.when(t < NT - 1)
    def _():
        send_v2.wait_send()
        forward.wait_send()

    @pl.when(jnp.logical_not(k_self))
    def _():
        send_k.wait_send()

    def end_r(j):
        own, copy, local = send_r(j)

        @pl.when(jnp.logical_not(own))
        def _():
            copy.wait_send()

    loop(SLABS, end_r)

    @pl.when(is_worker)
    def _():
        for dj in (-1, 0, 1):
            j = s + dj

            @pl.when((block < NT // BLOCK - 1) & (j >= 0) & (j < SLABS))
            def _(dj=dj):
                hand(dj).wait_send()

        def end_spread(h):
            def one(to):
                own, copy, local = spread(h, to)

                @pl.when(jnp.logical_not(own))
                def _():
                    copy.wait_send()

            loop(SLABS, one)

        loop(BLOCK, end_spread)


def body(nodes, coefficients):
    dma = pltpu.SemaphoreType.DMA
    fine = (DEPTH, ROWS, COLS)
    rimmed = (DEPTH + 2, ROWS + 2 * RIM, COLS)
    coarse = (DEPTH, HALF, LANES)
    scratch = [
        (7,) + fine, rimmed, rimmed, rimmed, fine, fine, fine,
        (7, DEPTH, HALF + 2 * RIM, LANES), (DEPTH, HALF + 2 * RIM, LANES), coarse, coarse,
        (7, 32, WIN, LANES), (BLOCK, 32, WIN, LANES), (BLOCK + 1, 34, WIN, LANES), coarse, coarse,
    ]
    sems = [(3, 2), (3, 2), (2,), (2,), (1,), (1,), (8,), (8,), (3,), (3,), (8, 8), (1,), (1,), (1,)]
    return pl.pallas_call(
        kernel,
        out_shape=jax.ShapeDtypeStruct(nodes.shape, F32),
        in_specs=[pl.BlockSpec(memory_space=pltpu.VMEM)] * 2,
        out_specs=pl.BlockSpec(memory_space=pltpu.VMEM),
        scratch_shapes=[pltpu.VMEM(shape, F32) for shape in scratch]
        + [dma(shape) for shape in sems]
        + [pltpu.SemaphoreType.REGULAR],
        compiler_params=pltpu.CompilerParams(
            collective_id=0, has_side_effects=True, vmem_limit_bytes=48 * 1024 * 1024
        ),
        name="pfasst",
    )(nodes, coefficients)


def solution(mesh):
    return jax.shard_map(
        body,
        mesh=mesh,
        in_specs=(P("tm", None, "space", None, None), P(None, "space", None, None)),
        out_specs=P("tm", None, "space", None, None),
        check_vma=False,
    )
```

```python
import functools

import jax
import jax.numpy as jnp
from jax import lax
from jax.experimental import pallas as pl
from jax.experimental.pallas import tpu as pltpu
from jax.sharding import PartitionSpec as P

MESH = pl.DeviceIdType.MESH
F32 = jnp.float32

A0, A1, A2 = 0.2 * 5.0 / 24.0, 0.2 / 3.0, -0.2 / 24.0
B0, B1, B2 = -0.2 / 24.0, 0.2 / 3.0, 0.2 * 5.0 / 24.0
C0, C1 = 0.2 / 6.0, 0.2 * 2.0 / 3.0

DEPTH = 4
ROWS, COLS = 128, 256
HALF, LANES = 64, 128
SLABS = 8
BLOCK = 8
NT = 32
RIM = 8
STRIP = 32
WIN = 24
DEEP = 24


def worker(half, j):
    odd = lax.rem(j, 2)
    return jnp.where(half == 0, 6 - 2 * odd, 2 * odd), j - odd + half


def neighbours(value, axis, size, mask_low, mask_high):
    ahead = pltpu.roll(value, size - 1, axis)
    behind = pltpu.roll(value, 1, axis)
    return jnp.where(mask_high, 0.0, ahead), jnp.where(mask_low, 0.0, behind)


def rows_around(value, size):
    return pltpu.roll(value, size - 1, 0), pltpu.roll(value, 1, 0)


def stencil(low, here, high, k, height, width, top, rows):
    lane = lax.broadcasted_iota(jnp.int32, (height, width), 1)
    first, last = lane == 0, lane == width - 1
    cut = lambda v: v[top : top + rows]
    over_z = high - low
    right, left = neighbours(here, 1, width, first, last)
    slope = right - left
    d_right, d_left = neighbours(over_z, 1, width, first, last)
    down, up = rows_around(here, height)
    z_down, z_up = rows_around(over_z, height)
    s_down, s_up = rows_around(slope, height)
    total = k[0] * cut(high + low) + k[1] * cut(down + up) + k[2] * cut(right + left)
    total = total + k[3] * cut(z_down - z_up) + k[4] * cut(d_right - d_left)
    total = total + k[5] * cut(s_down - s_up)
    return total + k[6] * cut(here)


def pair_matrix(shape, long_axis, value):
    long = lax.broadcasted_iota(jnp.int32, shape, long_axis)
    short = lax.broadcasted_iota(jnp.int32, shape, 1 - long_axis)
    return jnp.where((long == 2 * short) | (long == 2 * short + 1), value, 0.0).astype(jnp.bfloat16)


def times(value, matrix):
    high = value.astype(jnp.bfloat16)
    low = (value - high.astype(F32)).astype(jnp.bfloat16)
    dot = functools.partial(jnp.dot, preferred_element_type=F32)
    return dot(high, matrix) + dot(low, matrix)


def loop(count, fn, unroll=1):
    def step(i, carry):
        fn(i)
        return carry

    lax.fori_loop(0, count, step, 0, unroll=unroll)


def kernel(
    nodes, coeffs, out,
    kf, ab, bb, cb, v1, v2, v2p, kcp, rp, w0, wn, kb, rb, hb, ec, en, pairs, wide, narrow,
    halo_s, halo_r, shift_s, shift_r, k_s, k_r, r_s, r_r, hand_s, hand_r, e_s, e_r, f_s, f_r, known,
):
    t = lax.axis_index("tm")
    s = lax.axis_index("space")
    block = lax.div(t, BLOCK)
    place = lax.rem(t, BLOCK)
    base = block * BLOCK
    half = lax.rem(s, 2)
    turn = jnp.where(half == 0, 6 - place, place)
    is_worker = (turn == 0) | (turn == 2)
    chunk = s - half + lax.div(turn, 2)
    last_block = NT // BLOCK - 1
    strips = ROWS // STRIP

    def tell(sem, tm, sp):
        pl.semaphore_signal(sem, inc=1, device_id=(tm, sp), device_id_type=MESH)

    barrier = pltpu.get_barrier_semaphore()
    for n in range(1, SLABS):
        tell(barrier, t, lax.rem(s + n, SLABS))
    for n in range(1, BLOCK):
        tell(barrier, base + lax.rem(place + n, BLOCK), s)

    cross_up = (place == BLOCK - 1) & (t < NT - 1)
    cross_down = (place == 0) & (t > 0)

    @pl.when(cross_up)
    def _():
        tell(barrier, t + 1, s)

    @pl.when(cross_down)
    def _():
        tell(barrier, t - 1, s)

    for dj in (-1, 0, 1):
        j = chunk + dj

        @pl.when(is_worker & (block > 0) & (j >= 0) & (j < SLABS))
        def _(j=j):
            for z in (0, 1):
                to, at = worker(z, j)
                tell(barrier, base - BLOCK + to, at)

    for buf in (ab, bb, cb):
        buf[:, 0:RIM, :] = jnp.zeros((DEPTH + 2, RIM, COLS), F32)
        buf[:, RIM + ROWS :, :] = jnp.zeros((DEPTH + 2, RIM, COLS), F32)

    @pl.when(s == 0)
    def _():
        for buf in (ab, bb, cb):
            buf[0, RIM : RIM + ROWS, :] = jnp.zeros((ROWS, COLS), F32)

    @pl.when(s == SLABS - 1)
    def _():
        for buf in (ab, bb, cb):
            buf[DEPTH + 1, RIM : RIM + ROWS, :] = jnp.zeros((ROWS, COLS), F32)

    kcp[:, :, 0:RIM, :] = jnp.zeros((7, DEPTH, RIM, LANES), F32)
    kcp[:, :, RIM + HALF :, :] = jnp.zeros((7, DEPTH, RIM, LANES), F32)
    rp[:, 0:RIM, :] = jnp.zeros((DEPTH, RIM, LANES), F32)
    rp[:, RIM + HALF :, :] = jnp.zeros((DEPTH, RIM, LANES), F32)

    def combine_a(p, i):
        here = pl.ds(pl.multiple_of(i * STRIP, STRIP), STRIP)
        there = pl.ds(pl.multiple_of(RIM + i * STRIP, 8), STRIP)
        ab[p + 1, there, :] = A0 * nodes[0, 0, p, here, :] + A1 * nodes[0, 1, p, here, :] + A2 * nodes[0, 2, p, here, :]

    loop(strips, lambda i: combine_a(0, i))
    loop(strips, lambda i: combine_a(3, i))

    expect = 14 + jnp.where(cross_up, 1, 0) + jnp.where(cross_down, 1, 0)
    hands = 6 - jnp.where(chunk == 0, 2, 0) - jnp.where(chunk == SLABS - 1, 2, 0)
    expect = expect + jnp.where(is_worker & (block < last_block), hands, 0)
    pl.semaphore_wait(barrier, expect)

    inner = pl.ds(RIM, ROWS)

    def halo(buf, phase, upward):
        return pltpu.make_async_remote_copy(
            src_ref=buf.at[DEPTH if upward else 1, inner],
            dst_ref=buf.at[0 if upward else DEPTH + 1, inner],
            send_sem=halo_s.at[phase, int(upward)],
            recv_sem=halo_r.at[phase, int(upward)],
            device_id=(t, s + 1 if upward else s - 1),
            device_id_type=MESH,
        )

    def send_halo(buf, phase, upward):
        @pl.when(s < SLABS - 1 if upward else s > 0)
        def _():
            halo(buf, phase, upward).start()

    def take_halo(buf, phase, upward):
        @pl.when(s > 0 if upward else s < SLABS - 1)
        def _():
            halo(buf, phase, upward).wait_recv()

    send_halo(ab, 0, False)
    send_halo(ab, 0, True)
    for n in range(1, BLOCK):
        tell(known, base + lax.rem(place + n, BLOCK), s)

    narrow[...] = pair_matrix((COLS, LANES), 0, 0.25)
    wide[...] = pair_matrix((LANES, COLS), 1, 1.0)

    def restrict(p, across):
        pairs[p] = across
        return pairs[p, pl.ds(0, HALF, stride=2), :] + pairs[p, pl.ds(1, HALF, stride=2), :]

    def average(p, value):
        return restrict(p, times(value, narrow[...]))

    def prolong(p, value):
        pairs[p, pl.ds(0, HALF, stride=2), :] = value
        pairs[p, pl.ds(1, HALF, stride=2), :] = value
        return times(pairs[p], wide[...])

    def shift(src, dst, n, tm):
        return pltpu.make_async_remote_copy(
            src_ref=src, dst_ref=dst, send_sem=shift_s.at[n], recv_sem=shift_r.at[n],
            device_id=(tm, s), device_id_type=MESH,
        )

    send_w0 = shift(w0, wn, 0, t - 1)
    send_v2 = shift(v2, v2p, 1, t + 1)

    for p in range(DEPTH):
        w0[p] = average(p, nodes[0, 0, p])

    @pl.when(t > 0)
    def _():
        send_w0.start()

    @pl.when(t == NT - 1)
    def _():
        wn[...] = jnp.zeros_like(wn)

    def weights(p, i):
        here = pl.ds(pl.multiple_of(i * STRIP, STRIP), STRIP)
        k = [coeffs[m, p, here, :].astype(F32) for m in range(7)]
        for m in range(3):
            kf[m, p, here, :] = k[m]
            kf[3 + m, p, here, :] = 0.5 * k[3 + m]
        kf[6, p, here, :] = -(2.0 * (k[0] + k[1] + k[2]) + k[6])

    loop(DEPTH * strips, lambda n: weights(lax.div(n, strips), lax.rem(n, strips)))
    loop(strips, lambda i: combine_a(1, i))
    loop(strips, lambda i: combine_a(2, i))

    def force(buf, p, i):
        window = pl.ds(pl.multiple_of(i * STRIP, STRIP), STRIP + 2 * RIM)
        here = pl.ds(pl.multiple_of(i * STRIP, STRIP), STRIP)
        return stencil(
            buf[p, window, :], buf[p + 1, window, :], buf[p + 2, window, :],
            [kf[m, p, here, :] for m in range(7)], STRIP + 2 * RIM, COLS, RIM, STRIP,
        )

    def spots(i):
        return (
            pl.ds(pl.multiple_of(i * STRIP, STRIP), STRIP),
            pl.ds(pl.multiple_of(RIM + i * STRIP, 8), STRIP),
        )

    def first_node(p, i):
        here, there = spots(i)
        value = nodes[0, 0, p, here, :] + force(ab, p, i)
        v1[p, here, :] = value
        bb[p + 1, there, :] = (
            0.1 * value + B0 * nodes[0, 0, p, here, :] + (B1 - 0.1) * nodes[0, 1, p, here, :] + B2 * nodes[0, 2, p, here, :]
        )

    def last_node(p, i):
        here, there = spots(i)
        first = v1[p, here, :]
        value = first + force(bb, p, i)
        v2[p, here, :] = value
        cb[p + 1, there, :] = C0 * (nodes[0, 0, p, here, :] + value) + C1 * first

    def add_force(p, i):
        here, there = spots(i)
        out[0, 0, p, here, :] = nodes[0, 0, p, here, :] + force(cb, p, i)

    def planes(fn, which):
        for p in which:
            loop(strips, lambda i, p=p: fn(p, i))

    def coarse_weights(m):
        for p in range(DEPTH):
            across = jnp.dot(coeffs[m, p], narrow[...], preferred_element_type=F32)
            kcp[m, p, RIM : RIM + HALF, :] = restrict(p, across)

    loop(7, coarse_weights)

    def scale_weights(p):
        here = slice(RIM, RIM + HALF)
        k = [kcp[m, p, here, :] for m in range(7)]
        kcp[0, p, here, :] = 0.2 * k[0]
        for m in range(1, 5):
            kcp[m, p, here, :] = 0.05 * k[m]
        kcp[5, p, here, :] = 0.025 * k[5]
        kcp[6, p, here, :] = 1.0 - (0.4 * k[0] + 0.1 * (k[1] + k[2]) + 0.2 * k[6])

    loop(DEPTH, scale_weights)
    planes(first_node, (1, 2))
    pl.semaphore_wait(known, BLOCK - 1)

    window = pl.ds(pl.multiple_of(8 * place, 8), WIN)

    def send_k(z):
        to, at = worker(z, place)
        src, dst = kcp.at[:, :, window], kb.at[:, pl.ds(DEPTH * s - 8 * z, DEPTH)]
        own = (to == place) & (at == s)
        needed = s >= 2 if z else s <= 5
        copy = pltpu.make_async_remote_copy(
            src_ref=src, dst_ref=dst, send_sem=k_s.at[z], recv_sem=k_r.at[0],
            device_id=(base + to, at), device_id_type=MESH,
        )
        return needed & own, needed & jnp.logical_not(own), copy, pltpu.make_async_copy(src, dst, k_r.at[0])

    def start(parts):
        own, other, copy, local = parts

        @pl.when(own)
        def _():
            local.start()

        @pl.when(other)
        def _():
            copy.start()

    def end(parts):
        @pl.when(parts[1])
        def _():
            parts[2].wait_send()

    for z in (0, 1):
        start(send_k(z))

    take_halo(ab, 0, True)
    planes(first_node, (0,))
    send_halo(bb, 1, False)
    take_halo(ab, 0, False)
    planes(first_node, (3,))
    send_halo(bb, 1, True)
    planes(last_node, (1, 2))
    take_halo(bb, 1, True)
    planes(last_node, (0,))
    send_halo(cb, 2, False)
    take_halo(bb, 1, False)
    planes(last_node, (3,))
    send_halo(cb, 2, True)

    @pl.when(t < NT - 1)
    def _():
        send_v2.start()

    planes(add_force, (1, 2))
    take_halo(cb, 2, True)
    planes(add_force, (0,))
    take_halo(cb, 2, False)
    planes(add_force, (3,))

    @pl.when(t < NT - 1)
    def _():
        send_w0.wait_recv()

    for p in range(DEPTH):
        rp[p, RIM : RIM + HALF, :] = average(p, out[0, 0, p]) - wn[p]

    def send_r(z, j):
        to, at = worker(z, j)
        src = rp.at[:, pl.ds(pl.multiple_of(8 * j, 8), WIN)]
        dst = rb.at[place, pl.ds(DEPTH * s - 8 * z, DEPTH)]
        own = (to == place) & (at == s)
        needed = DEPTH * s + 3 >= 9 + place if z else DEPTH * s < 23 - place
        copy = pltpu.make_async_remote_copy(
            src_ref=src, dst_ref=dst, send_sem=r_s.at[z, j], recv_sem=r_r.at[place, s],
            device_id=(base + to, at), device_id_type=MESH,
        )
        return needed & own, needed & jnp.logical_not(own), copy, pltpu.make_async_copy(src, dst, r_r.at[place, s])

    for z in (0, 1):
        loop(SLABS, lambda j, z=z: start(send_r(z, j)))

    @pl.when(t > 0)
    def _():
        send_v2.wait_recv()

    @pl.when(t > 0)
    def _():
        for p in range(DEPTH):
            out[0, 0, p] = v2p[p] + prolong(p, average(p, nodes[0, 0, p] - v2p[p]))

    @pl.when(t == 0)
    def _():
        out[0, 0] = nodes[0, 0]

    for p in range(DEPTH):
        gap = prolong(p, wn[p] - average(p, v2[p]))
        out[0, 1, p] = v1[p] + 0.5 * gap
        out[0, 2, p] = v2[p] + gap

    def hand(z, dj):
        count = 8 if z else 16
        source = 9 if z else 1 + 8 * half
        target = jnp.where(half == 0, 1, 17) if z else source
        to, at = worker(1 - half if z else half, chunk + dj)
        return pltpu.make_async_remote_copy(
            src_ref=hb.at[BLOCK, pl.ds(source, count), pl.ds(8, 8)],
            dst_ref=hb.at[0, pl.ds(target, count), pl.ds(8 - 8 * dj, 8)],
            send_sem=hand_s.at[z, dj + 1],
            recv_sem=hand_r.at[z, dj + 1],
            device_id=(base + BLOCK + to, at),
            device_id_type=MESH,
        )

    def spread(h, n):
        to = 4 * half + n
        src = hb.at[h + 1, pl.ds(1 + 8 * half + DEPTH * n, DEPTH), pl.ds(8, 8)]
        dst = en.at[:, pl.ds(pl.multiple_of(8 * chunk, 8), 8)]
        own = (h == place) & (to == s)
        copy = pltpu.make_async_remote_copy(
            src_ref=src, dst_ref=dst, send_sem=e_s.at[h, n], recv_sem=e_r.at[0],
            device_id=(base + h, to), device_id_type=MESH,
        )
        return own, jnp.logical_not(own), copy, pltpu.make_async_copy(src, dst, e_r.at[0])

    def start_spread(h):
        loop(4, lambda n: start(spread(h, n)))

    @pl.when(is_worker)
    def _():
        def clear(h):
            hb[h, 0] = jnp.zeros((WIN, LANES), F32)
            hb[h, DEEP + 1] = jnp.zeros((WIN, LANES), F32)

        loop(BLOCK + 1, clear)

        @pl.when(block == 0)
        def _():
            hb[0, 1 : DEEP + 1] = jnp.zeros((DEEP, WIN, LANES), F32)

        @pl.when((block > 0) & (chunk == 0))
        def _():
            hb[0, 1 : DEEP + 1, 0:8, :] = jnp.zeros((DEEP, 8, LANES), F32)

        @pl.when((block > 0) & (chunk == SLABS - 1))
        def _():
            hb[0, 1 : DEEP + 1, 16:24, :] = jnp.zeros((DEEP, 8, LANES), F32)

        pltpu.make_async_copy(kb, kb, k_r.at[0]).wait()
        for dj in (-1, 0, 1):
            @pl.when((block > 0) & (chunk - dj >= 0) & (chunk - dj < SLABS))
            def _(dj=dj):
                hand(0, dj).wait_recv()
                hand(1, dj).wait_recv()

        lane = lax.broadcasted_iota(jnp.int32, (WIN, LANES), 1)
        first, last = lane == 0, lane == LANES - 1

        def slopes(v):
            right, left = neighbours(v, 1, LANES, first, last)
            down, up = rows_around(v, WIN)
            over_y = right - left
            s_down, s_up = rows_around(over_y, WIN)
            return v, over_y, down - up, right + left, down + up, s_down - s_up

        def advance(h):
            count = lax.div(26 - h, 4)
            slab0 = half * (SLABS - count)
            start_plane = DEPTH * slab0 - 8 * half

            def arrived(i):
                part = rb.at[h, pl.ds(start_plane + DEPTH * i, DEPTH)]
                pltpu.make_async_copy(part, part, r_r.at[h, slab0 + i]).wait()

            loop(count, arrived)
            low, low_y, low_x = slopes(hb[h, start_plane])[:3]

            def group(i, carry):
                (low, low_y, low_x), here = carry
                for n in range(DEPTH):
                    p = start_plane + DEPTH * i + n
                    above = slopes(hb[h, p + 2])
                    v, v_y, v_x, around_y, around_x, v_xy = here
                    total = rb[h, p] + kb[0, p] * (above[0] + low) + kb[1, p] * around_x + kb[2, p] * around_y
                    total = total + kb[3, p] * (above[2] - low_x) + kb[4, p] * (above[1] - low_y)
                    hb[h + 1, p + 1] = total + kb[5, p] * v_xy + kb[6, p] * v
                    low, low_y, low_x = v, v_y, v_x
                    here = above
                return (low, low_y, low_x), here

            lax.fori_loop(0, count, group, ((low, low_y, low_x), slopes(hb[h, start_plane + 1])))

            @pl.when(block == last_block)
            def _():
                start_spread(h)

        loop(BLOCK, advance)

        @pl.when(block < last_block)
        def _():
            for dj in (-1, 0, 1):
                j = chunk + dj

                @pl.when((j >= 0) & (j < SLABS))
                def _(dj=dj):
                    hand(0, dj).start()
                    hand(1, dj).start()

            loop(BLOCK, start_spread)

    pltpu.make_async_copy(en, en, e_r.at[0]).wait()
    forward = pltpu.make_async_remote_copy(
        src_ref=en, dst_ref=ec, send_sem=f_s.at[0], recv_sem=f_r.at[0], device_id=(t + 1, s), device_id_type=MESH
    )

    @pl.when(t < NT - 1)
    def _():
        forward.start()

    for p in range(DEPTH):
        gain = prolong(p, en[p])
        out[0, 2, p] += gain
        out[0, 1, p] += 0.5 * gain

    @pl.when(t > 0)
    def _():
        forward.wait_recv()

        for p in range(DEPTH):
            gain = prolong(p, ec[p])
            out[0, 0, p] += gain
            out[0, 1, p] += 0.5 * gain

    for phase, buf in enumerate((ab, bb, cb)):

        @pl.when(s < SLABS - 1)
        def _(phase=phase, buf=buf):
            halo(buf, phase, True).wait_send()

        @pl.when(s > 0)
        def _(phase=phase, buf=buf):
            halo(buf, phase, False).wait_send()

    @pl.when(t > 0)
    def _():
        send_w0.wait_send()

    @pl.when(t < NT - 1)
    def _():
        send_v2.wait_send()
        forward.wait_send()

    for z in (0, 1):
        end(send_k(z))
        loop(SLABS, lambda j, z=z: end(send_r(z, j)))

    @pl.when(is_worker)
    def _():
        for dj in (-1, 0, 1):
            j = chunk + dj

            @pl.when((block < last_block) & (j >= 0) & (j < SLABS))
            def _(dj=dj):
                hand(0, dj).wait_send()
                hand(1, dj).wait_send()

        def end_spread(h):
            loop(4, lambda n: end(spread(h, n)))

        loop(BLOCK, end_spread)


def body(nodes, coefficients):
    dma = pltpu.SemaphoreType.DMA
    fine = (DEPTH, ROWS, COLS)
    rimmed = (DEPTH + 2, ROWS + 2 * RIM, COLS)
    coarse = (DEPTH, HALF, LANES)
    scratch = [
        (7,) + fine, rimmed, rimmed, rimmed, fine, fine, fine,
        (7, DEPTH, HALF + 2 * RIM, LANES), (DEPTH, HALF + 2 * RIM, LANES), coarse, coarse,
        (7, DEEP, WIN, LANES), (BLOCK, DEEP, WIN, LANES), (BLOCK + 1, DEEP + 2, WIN, LANES), coarse, coarse,
        (DEPTH, ROWS, LANES),
    ]
    sems = [(3, 2), (3, 2), (2,), (2,), (2,), (1,), (2, 8), (8, 8), (2, 3), (2, 3), (8, 4), (1,), (1,), (1,)]
    return pl.pallas_call(
        kernel,
        out_shape=jax.ShapeDtypeStruct(nodes.shape, F32),
        in_specs=[pl.BlockSpec(memory_space=pltpu.VMEM)] * 2,
        out_specs=pl.BlockSpec(memory_space=pltpu.VMEM),
        scratch_shapes=[pltpu.VMEM(shape, F32) for shape in scratch]
        + [pltpu.VMEM((LANES, COLS), jnp.bfloat16), pltpu.VMEM((COLS, LANES), jnp.bfloat16)]
        + [dma(shape) for shape in sems]
        + [pltpu.SemaphoreType.REGULAR],
        compiler_params=pltpu.CompilerParams(
            collective_id=0, has_side_effects=True, vmem_limit_bytes=48 * 1024 * 1024
        ),
        name="pfasst",
    )(nodes, coefficients)


def solution(mesh):
    return jax.shard_map(
        body,
        mesh=mesh,
        in_specs=(P("tm", None, "space", None, None), P(None, "space", None, None)),
        out_specs=P("tm", None, "space", None, None),
        check_vma=False,
    )
```

```python
import functools

import jax
import jax.numpy as jnp
from jax import lax
from jax.experimental import pallas as pl
from jax.experimental.pallas import tpu as pltpu
from jax.sharding import PartitionSpec as P

MESH = pl.DeviceIdType.MESH
F32 = jnp.float32

A0, A1, A2 = 0.2 * 5.0 / 24.0, 0.2 / 3.0, -0.2 / 24.0
B0, B1, B2 = -0.2 / 24.0, 0.2 / 3.0, 0.2 * 5.0 / 24.0
C0, C1 = 0.2 / 6.0, 0.2 * 2.0 / 3.0

DEPTH = 4
ROWS, COLS = 128, 256
HALF, LANES = 64, 128
SLABS = 8
BLOCK = 8
NT = 32
RIM = 8
STRIP = 32
WIN = 24
DEEP = 24


def worker(half, j):
    odd = lax.rem(j, 2)
    return 2 * lax.rem(j, 4), 2 * jnp.where(half == 0, odd, 3 - odd) + lax.div(j, 4)


def neighbours(value, axis, size, mask_low, mask_high):
    ahead = pltpu.roll(value, size - 1, axis)
    behind = pltpu.roll(value, 1, axis)
    return jnp.where(mask_high, 0.0, ahead), jnp.where(mask_low, 0.0, behind)


def rows_around(value, size):
    return pltpu.roll(value, size - 1, 0), pltpu.roll(value, 1, 0)


def stencil(low, here, high, k, height, width, top, rows):
    lane = lax.broadcasted_iota(jnp.int32, (height, width), 1)
    first, last = lane == 0, lane == width - 1
    cut = lambda v: v[top : top + rows]
    over_z = high - low
    right, left = neighbours(here, 1, width, first, last)
    slope = right - left
    d_right, d_left = neighbours(over_z, 1, width, first, last)
    down, up = rows_around(here, height)
    z_down, z_up = rows_around(over_z, height)
    s_down, s_up = rows_around(slope, height)
    total = k[0] * cut(high + low) + k[1] * cut(down + up) + k[2] * cut(right + left)
    total = total + k[3] * cut(z_down - z_up) + k[4] * cut(d_right - d_left)
    total = total + k[5] * cut(s_down - s_up)
    return total + k[6] * cut(here)


def pair_matrix(shape, long_axis, value):
    long = lax.broadcasted_iota(jnp.int32, shape, long_axis)
    short = lax.broadcasted_iota(jnp.int32, shape, 1 - long_axis)
    return jnp.where((long == 2 * short) | (long == 2 * short + 1), value, 0.0).astype(jnp.bfloat16)


def times(value, matrix):
    high = value.astype(jnp.bfloat16)
    low = (value - high.astype(F32)).astype(jnp.bfloat16)
    dot = functools.partial(jnp.dot, preferred_element_type=F32)
    return dot(high, matrix) + dot(low, matrix)


def loop(count, fn, unroll=1):
    def step(i, carry):
        fn(i)
        return carry

    lax.fori_loop(0, count, step, 0, unroll=unroll)


def kernel(
    nodes, coeffs, out,
    kf, ab, bb, cb, v1, v2, v2p, kcp, rp, w0, wn, kb, rb, hb, ec, en, pairs, wide, narrow,
    halo_s, halo_r, shift_s, shift_r, k_s, k_r, r_s, r_r, hand_s, hand_r, e_s, e_r, f_s, f_r, known,
):
    t = lax.axis_index("tm")
    s = lax.axis_index("space")
    block = lax.div(t, BLOCK)
    place = lax.rem(t, BLOCK)
    base = block * BLOCK
    half = lax.div(s, 4)
    chunk = 4 * lax.rem(s, 2) + lax.div(place, 2)
    odd = lax.rem(lax.div(s, 2), 2)
    is_worker = (lax.rem(place, 2) == 0) & (lax.rem(chunk, 2) == jnp.where(half == 0, odd, 1 - odd))
    last_block = NT // BLOCK - 1
    strips = ROWS // STRIP

    def tell(sem, tm, sp):
        pl.semaphore_signal(sem, inc=1, device_id=(tm, sp), device_id_type=MESH)

    barrier = pltpu.get_barrier_semaphore()
    for n in range(1, SLABS):
        tell(barrier, t, lax.rem(s + n, SLABS))
    for n in range(1, BLOCK):
        tell(barrier, base + lax.rem(place + n, BLOCK), s)

    cross_up = (place == BLOCK - 1) & (t < NT - 1)
    cross_down = (place == 0) & (t > 0)

    @pl.when(cross_up)
    def _():
        tell(barrier, t + 1, s)

    @pl.when(cross_down)
    def _():
        tell(barrier, t - 1, s)

    for dj in (-1, 0, 1):
        j = chunk + dj

        @pl.when(is_worker & (block > 0) & (j >= 0) & (j < SLABS))
        def _(j=j):
            for z in (0, 1):
                to, at = worker(z, j)
                tell(barrier, base - BLOCK + to, at)

    for buf in (ab, bb, cb):
        buf[:, 0:RIM, :] = jnp.zeros((DEPTH + 2, RIM, COLS), F32)
        buf[:, RIM + ROWS :, :] = jnp.zeros((DEPTH + 2, RIM, COLS), F32)

    @pl.when(s == 0)
    def _():
        for buf in (ab, bb, cb):
            buf[0, RIM : RIM + ROWS, :] = jnp.zeros((ROWS, COLS), F32)

    @pl.when(s == SLABS - 1)
    def _():
        for buf in (ab, bb, cb):
            buf[DEPTH + 1, RIM : RIM + ROWS, :] = jnp.zeros((ROWS, COLS), F32)

    kcp[:, :, 0:RIM, :] = jnp.zeros((7, DEPTH, RIM, LANES), F32)
    kcp[:, :, RIM + HALF :, :] = jnp.zeros((7, DEPTH, RIM, LANES), F32)
    rp[:, 0:RIM, :] = jnp.zeros((DEPTH, RIM, LANES), F32)
    rp[:, RIM + HALF :, :] = jnp.zeros((DEPTH, RIM, LANES), F32)

    def combine_a(p, i):
        here = pl.ds(pl.multiple_of(i * STRIP, STRIP), STRIP)
        there = pl.ds(pl.multiple_of(RIM + i * STRIP, 8), STRIP)
        ab[p + 1, there, :] = A0 * nodes[0, 0, p, here, :] + A1 * nodes[0, 1, p, here, :] + A2 * nodes[0, 2, p, here, :]

    loop(strips, lambda i: combine_a(0, i))
    loop(strips, lambda i: combine_a(3, i))

    expect = 14 + jnp.where(cross_up, 1, 0) + jnp.where(cross_down, 1, 0)
    hands = 6 - jnp.where(chunk == 0, 2, 0) - jnp.where(chunk == SLABS - 1, 2, 0)
    expect = expect + jnp.where(is_worker & (block < last_block), hands, 0)
    pl.semaphore_wait(barrier, expect)

    inner = pl.ds(RIM, ROWS)

    def halo(buf, phase, upward):
        return pltpu.make_async_remote_copy(
            src_ref=buf.at[DEPTH if upward else 1, inner],
            dst_ref=buf.at[0 if upward else DEPTH + 1, inner],
            send_sem=halo_s.at[phase, int(upward)],
            recv_sem=halo_r.at[phase, int(upward)],
            device_id=(t, s + 1 if upward else s - 1),
            device_id_type=MESH,
        )

    def send_halo(buf, phase, upward):
        @pl.when(s < SLABS - 1 if upward else s > 0)
        def _():
            halo(buf, phase, upward).start()

    def take_halo(buf, phase, upward):
        @pl.when(s > 0 if upward else s < SLABS - 1)
        def _():
            halo(buf, phase, upward).wait_recv()

    send_halo(ab, 0, False)
    send_halo(ab, 0, True)
    for n in range(1, BLOCK):
        tell(known, base + lax.rem(place + n, BLOCK), s)

    narrow[...] = pair_matrix((COLS, LANES), 0, 0.25)
    wide[...] = pair_matrix((LANES, COLS), 1, 1.0)

    def restrict(p, across):
        pairs[p] = across
        return pairs[p, pl.ds(0, HALF, stride=2), :] + pairs[p, pl.ds(1, HALF, stride=2), :]

    def average(p, value):
        return restrict(p, times(value, narrow[...]))

    def prolong(p, value):
        pairs[p, pl.ds(0, HALF, stride=2), :] = value
        pairs[p, pl.ds(1, HALF, stride=2), :] = value
        return times(pairs[p], wide[...])

    def shift(src, dst, n, tm):
        return pltpu.make_async_remote_copy(
            src_ref=src, dst_ref=dst, send_sem=shift_s.at[n], recv_sem=shift_r.at[n],
            device_id=(tm, s), device_id_type=MESH,
        )

    send_w0 = shift(w0, wn, 0, t - 1)
    send_v2 = shift(v2, v2p, 1, t + 1)

    for p in range(DEPTH):
        w0[p] = average(p, nodes[0, 0, p])

    @pl.when(t > 0)
    def _():
        send_w0.start()

    @pl.when(t == NT - 1)
    def _():
        wn[...] = jnp.zeros_like(wn)

    def weights(p, i):
        here = pl.ds(pl.multiple_of(i * STRIP, STRIP), STRIP)
        k = [coeffs[m, p, here, :].astype(F32) for m in range(7)]
        for m in range(3):
            kf[m, p, here, :] = k[m]
            kf[3 + m, p, here, :] = 0.5 * k[3 + m]
        kf[6, p, here, :] = -(2.0 * (k[0] + k[1] + k[2]) + k[6])

    loop(DEPTH * strips, lambda n: weights(lax.div(n, strips), lax.rem(n, strips)))
    loop(strips, lambda i: combine_a(1, i))
    loop(strips, lambda i: combine_a(2, i))

    def force(buf, p, i):
        window = pl.ds(pl.multiple_of(i * STRIP, STRIP), STRIP + 2 * RIM)
        here = pl.ds(pl.multiple_of(i * STRIP, STRIP), STRIP)
        return stencil(
            buf[p, window, :], buf[p + 1, window, :], buf[p + 2, window, :],
            [kf[m, p, here, :] for m in range(7)], STRIP + 2 * RIM, COLS, RIM, STRIP,
        )

    def spots(i):
        return (
            pl.ds(pl.multiple_of(i * STRIP, STRIP), STRIP),
            pl.ds(pl.multiple_of(RIM + i * STRIP, 8), STRIP),
        )

    def first_node(p, i):
        here, there = spots(i)
        value = nodes[0, 0, p, here, :] + force(ab, p, i)
        v1[p, here, :] = value
        bb[p + 1, there, :] = (
            0.1 * value + B0 * nodes[0, 0, p, here, :] + (B1 - 0.1) * nodes[0, 1, p, here, :] + B2 * nodes[0, 2, p, here, :]
        )

    def last_node(p, i):
        here, there = spots(i)
        first = v1[p, here, :]
        value = first + force(bb, p, i)
        v2[p, here, :] = value
        cb[p + 1, there, :] = C0 * (nodes[0, 0, p, here, :] + value) + C1 * first

    def add_force(p, i):
        here, there = spots(i)
        out[0, 0, p, here, :] = nodes[0, 0, p, here, :] + force(cb, p, i)

    def planes(fn, which):
        for p in which:
            loop(strips, lambda i, p=p: fn(p, i))

    def coarse_weights(m):
        for p in range(DEPTH):
            across = jnp.dot(coeffs[m, p], narrow[...], preferred_element_type=F32)
            kcp[m, p, RIM : RIM + HALF, :] = restrict(p, across)

    loop(7, coarse_weights)

    def scale_weights(p):
        here = slice(RIM, RIM + HALF)
        k = [kcp[m, p, here, :] for m in range(7)]
        kcp[0, p, here, :] = 0.2 * k[0]
        for m in range(1, 5):
            kcp[m, p, here, :] = 0.05 * k[m]
        kcp[5, p, here, :] = 0.025 * k[5]
        kcp[6, p, here, :] = 1.0 - (0.4 * k[0] + 0.1 * (k[1] + k[2]) + 0.2 * k[6])

    loop(DEPTH, scale_weights)
    planes(first_node, (1, 2))
    pl.semaphore_wait(known, BLOCK - 1)

    window = pl.ds(pl.multiple_of(8 * place, 8), WIN)

    def send_k(z):
        to, at = worker(z, place)
        src, dst = kcp.at[:, :, window], kb.at[:, pl.ds(DEPTH * s - 8 * z, DEPTH)]
        own = (to == place) & (at == s)
        needed = s >= 2 if z else s <= 5
        copy = pltpu.make_async_remote_copy(
            src_ref=src, dst_ref=dst, send_sem=k_s.at[z], recv_sem=k_r.at[0],
            device_id=(base + to, at), device_id_type=MESH,
        )
        return needed & own, needed & jnp.logical_not(own), copy, pltpu.make_async_copy(src, dst, k_r.at[0])

    def start(parts):
        own, other, copy, local = parts

        @pl.when(own)
        def _():
            local.start()

        @pl.when(other)
        def _():
            copy.start()

    def end(parts):
        @pl.when(parts[1])
        def _():
            parts[2].wait_send()

    for z in (0, 1):
        start(send_k(z))

    take_halo(ab, 0, True)
    planes(first_node, (0,))
    send_halo(bb, 1, False)
    take_halo(ab, 0, False)
    planes(first_node, (3,))
    send_halo(bb, 1, True)
    planes(last_node, (1, 2))
    take_halo(bb, 1, True)
    planes(last_node, (0,))
    send_halo(cb, 2, False)
    take_halo(bb, 1, False)
    planes(last_node, (3,))
    send_halo(cb, 2, True)

    @pl.when(t < NT - 1)
    def _():
        send_v2.start()

    planes(add_force, (1, 2))
    take_halo(cb, 2, True)
    planes(add_force, (0,))
    take_halo(cb, 2, False)
    planes(add_force, (3,))

    @pl.when(t < NT - 1)
    def _():
        send_w0.wait_recv()

    for p in range(DEPTH):
        rp[p, RIM : RIM + HALF, :] = average(p, out[0, 0, p]) - wn[p]

    def send_r(z, j):
        to, at = worker(z, j)
        src = rp.at[:, pl.ds(pl.multiple_of(8 * j, 8), WIN)]
        dst = rb.at[place, pl.ds(DEPTH * s - 8 * z, DEPTH)]
        own = (to == place) & (at == s)
        needed = DEPTH * s + 3 >= 9 + place if z else DEPTH * s < 23 - place
        copy = pltpu.make_async_remote_copy(
            src_ref=src, dst_ref=dst, send_sem=r_s.at[z, j], recv_sem=r_r.at[place, s],
            device_id=(base + to, at), device_id_type=MESH,
        )
        return needed & own, needed & jnp.logical_not(own), copy, pltpu.make_async_copy(src, dst, r_r.at[place, s])

    for z in (0, 1):
        loop(SLABS, lambda j, z=z: start(send_r(z, j)))

    @pl.when(t > 0)
    def _():
        send_v2.wait_recv()

    @pl.when(t > 0)
    def _():
        for p in range(DEPTH):
            out[0, 0, p] = v2p[p] + prolong(p, average(p, nodes[0, 0, p] - v2p[p]))

    @pl.when(t == 0)
    def _():
        out[0, 0] = nodes[0, 0]

    for p in range(DEPTH):
        gap = prolong(p, wn[p] - average(p, v2[p]))
        out[0, 1, p] = v1[p] + 0.5 * gap
        out[0, 2, p] = v2[p] + gap

    def hand(z, dj):
        count = 8 if z else 16
        source = 9 if z else 1 + 8 * half
        target = jnp.where(half == 0, 1, 17) if z else source
        to, at = worker(1 - half if z else half, chunk + dj)
        return pltpu.make_async_remote_copy(
            src_ref=hb.at[BLOCK, pl.ds(source, count), pl.ds(8, 8)],
            dst_ref=hb.at[0, pl.ds(target, count), pl.ds(8 - 8 * dj, 8)],
            send_sem=hand_s.at[z, dj + 1],
            recv_sem=hand_r.at[z, dj + 1],
            device_id=(base + BLOCK + to, at),
            device_id_type=MESH,
        )

    def spread(h, n):
        to = 4 * half + n
        src = hb.at[h + 1, pl.ds(1 + 8 * half + DEPTH * n, DEPTH), pl.ds(8, 8)]
        dst = en.at[:, pl.ds(pl.multiple_of(8 * chunk, 8), 8)]
        own = (h == place) & (to == s)
        copy = pltpu.make_async_remote_copy(
            src_ref=src, dst_ref=dst, send_sem=e_s.at[h, n], recv_sem=e_r.at[0],
            device_id=(base + h, to), device_id_type=MESH,
        )
        return own, jnp.logical_not(own), copy, pltpu.make_async_copy(src, dst, e_r.at[0])

    def start_spread(h):
        loop(4, lambda n: start(spread(h, n)))

    @pl.when(is_worker)
    def _():
        def clear(h):
            hb[h, 0] = jnp.zeros((WIN, LANES), F32)
            hb[h, DEEP + 1] = jnp.zeros((WIN, LANES), F32)

        loop(BLOCK + 1, clear)

        @pl.when(block == 0)
        def _():
            hb[0, 1 : DEEP + 1] = jnp.zeros((DEEP, WIN, LANES), F32)

        @pl.when((block > 0) & (chunk == 0))
        def _():
            hb[0, 1 : DEEP + 1, 0:8, :] = jnp.zeros((DEEP, 8, LANES), F32)

        @pl.when((block > 0) & (chunk == SLABS - 1))
        def _():
            hb[0, 1 : DEEP + 1, 16:24, :] = jnp.zeros((DEEP, 8, LANES), F32)

        pltpu.make_async_copy(kb, kb, k_r.at[0]).wait()
        for dj in (-1, 0, 1):
            @pl.when((block > 0) & (chunk - dj >= 0) & (chunk - dj < SLABS))
            def _(dj=dj):
                hand(0, dj).wait_recv()
                hand(1, dj).wait_recv()

        lane = lax.broadcasted_iota(jnp.int32, (WIN, LANES), 1)
        first, last = lane == 0, lane == LANES - 1

        def slopes(v):
            right, left = neighbours(v, 1, LANES, first, last)
            down, up = rows_around(v, WIN)
            over_y = right - left
            s_down, s_up = rows_around(over_y, WIN)
            return v, over_y, down - up, right + left, down + up, s_down - s_up

        def advance(h):
            count = lax.div(26 - h, 4)
            slab0 = half * (SLABS - count)
            start_plane = DEPTH * slab0 - 8 * half

            def arrived(i):
                part = rb.at[h, pl.ds(start_plane + DEPTH * i, DEPTH)]
                pltpu.make_async_copy(part, part, r_r.at[h, slab0 + i]).wait()

            loop(count, arrived)
            low, low_y, low_x = slopes(hb[h, start_plane])[:3]

            def group(i, carry):
                (low, low_y, low_x), here = carry
                for n in range(DEPTH):
                    p = start_plane + DEPTH * i + n
                    above = slopes(hb[h, p + 2])
                    v, v_y, v_x, around_y, around_x, v_xy = here
                    total = rb[h, p] + kb[0, p] * (above[0] + low) + kb[1, p] * around_x + kb[2, p] * around_y
                    total = total + kb[3, p] * (above[2] - low_x) + kb[4, p] * (above[1] - low_y)
                    hb[h + 1, p + 1] = total + kb[5, p] * v_xy + kb[6, p] * v
                    low, low_y, low_x = v, v_y, v_x
                    here = above
                return (low, low_y, low_x), here

            lax.fori_loop(0, count, group, ((low, low_y, low_x), slopes(hb[h, start_plane + 1])))

            @pl.when(block == last_block)
            def _():
                start_spread(h)

        loop(BLOCK, advance)

        @pl.when(block < last_block)
        def _():
            for dj in (-1, 0, 1):
                j = chunk + dj

                @pl.when((j >= 0) & (j < SLABS))
                def _(dj=dj):
                    hand(0, dj).start()
                    hand(1, dj).start()

            loop(BLOCK, start_spread)

    pltpu.make_async_copy(en, en, e_r.at[0]).wait()
    forward = pltpu.make_async_remote_copy(
        src_ref=en, dst_ref=ec, send_sem=f_s.at[0], recv_sem=f_r.at[0], device_id=(t + 1, s), device_id_type=MESH
    )

    @pl.when(t < NT - 1)
    def _():
        forward.start()

    for p in range(DEPTH):
        gain = prolong(p, en[p])
        out[0, 2, p] += gain
        out[0, 1, p] += 0.5 * gain

    @pl.when(t > 0)
    def _():
        forward.wait_recv()

        for p in range(DEPTH):
            gain = prolong(p, ec[p])
            out[0, 0, p] += gain
            out[0, 1, p] += 0.5 * gain

    for phase, buf in enumerate((ab, bb, cb)):

        @pl.when(s < SLABS - 1)
        def _(phase=phase, buf=buf):
            halo(buf, phase, True).wait_send()

        @pl.when(s > 0)
        def _(phase=phase, buf=buf):
            halo(buf, phase, False).wait_send()

    @pl.when(t > 0)
    def _():
        send_w0.wait_send()

    @pl.when(t < NT - 1)
    def _():
        send_v2.wait_send()
        forward.wait_send()

    for z in (0, 1):
        end(send_k(z))
        loop(SLABS, lambda j, z=z: end(send_r(z, j)))

    @pl.when(is_worker)
    def _():
        for dj in (-1, 0, 1):
            j = chunk + dj

            @pl.when((block < last_block) & (j >= 0) & (j < SLABS))
            def _(dj=dj):
                hand(0, dj).wait_send()
                hand(1, dj).wait_send()

        def end_spread(h):
            loop(4, lambda n: end(spread(h, n)))

        loop(BLOCK, end_spread)


def body(nodes, coefficients):
    dma = pltpu.SemaphoreType.DMA
    fine = (DEPTH, ROWS, COLS)
    rimmed = (DEPTH + 2, ROWS + 2 * RIM, COLS)
    coarse = (DEPTH, HALF, LANES)
    scratch = [
        (7,) + fine, rimmed, rimmed, rimmed, fine, fine, fine,
        (7, DEPTH, HALF + 2 * RIM, LANES), (DEPTH, HALF + 2 * RIM, LANES), coarse, coarse,
        (7, DEEP, WIN, LANES), (BLOCK, DEEP, WIN, LANES), (BLOCK + 1, DEEP + 2, WIN, LANES), coarse, coarse,
        (DEPTH, ROWS, LANES),
    ]
    sems = [(3, 2), (3, 2), (2,), (2,), (2,), (1,), (2, 8), (8, 8), (2, 3), (2, 3), (8, 4), (1,), (1,), (1,)]
    return pl.pallas_call(
        kernel,
        out_shape=jax.ShapeDtypeStruct(nodes.shape, F32),
        in_specs=[pl.BlockSpec(memory_space=pltpu.VMEM)] * 2,
        out_specs=pl.BlockSpec(memory_space=pltpu.VMEM),
        scratch_shapes=[pltpu.VMEM(shape, F32) for shape in scratch]
        + [pltpu.VMEM((LANES, COLS), jnp.bfloat16), pltpu.VMEM((COLS, LANES), jnp.bfloat16)]
        + [dma(shape) for shape in sems]
        + [pltpu.SemaphoreType.REGULAR],
        compiler_params=pltpu.CompilerParams(
            collective_id=0, has_side_effects=True, vmem_limit_bytes=48 * 1024 * 1024
        ),
        name="pfasst",
    )(nodes, coefficients)


def solution(mesh):
    return jax.shard_map(
        body,
        mesh=mesh,
        in_specs=(P("tm", None, "space", None, None), P(None, "space", None, None)),
        out_specs=P("tm", None, "space", None, None),
        check_vma=False,
    )
```

```python
import functools

import jax
import jax.numpy as jnp
from jax import lax
from jax.experimental import pallas as pl
from jax.experimental.pallas import tpu as pltpu
from jax.sharding import PartitionSpec as P

MESH = pl.DeviceIdType.MESH
F32 = jnp.float32

A0, A1, A2 = 0.2 * 5.0 / 24.0, 0.2 / 3.0, -0.2 / 24.0
B0, B1, B2 = -0.2 / 24.0, 0.2 / 3.0, 0.2 * 5.0 / 24.0
C0, C1 = 0.2 / 6.0, 0.2 * 2.0 / 3.0

DEPTH = 4
ROWS, COLS = 128, 256
HALF, LANES = 64, 128
SLABS = 8
BLOCK = 8
NT = 32
RIM = 8
STRIP = 32
WIN = 24
DEEP = 24


def worker(half, j):
    odd = lax.rem(j, 2)
    return 2 * lax.rem(j, 4), 2 * jnp.where(half == 0, odd, 3 - odd) + lax.div(j, 4)


def neighbours(value, axis, size, mask_low, mask_high):
    ahead = pltpu.roll(value, size - 1, axis)
    behind = pltpu.roll(value, 1, axis)
    return jnp.where(mask_high, 0.0, ahead), jnp.where(mask_low, 0.0, behind)


def rows_around(value, size):
    return pltpu.roll(value, size - 1, 0), pltpu.roll(value, 1, 0)


def stencil(low, here, high, k, height, width, top, rows):
    lane = lax.broadcasted_iota(jnp.int32, (height, width), 1)
    first, last = lane == 0, lane == width - 1
    cut = lambda v: v[top : top + rows]
    over_z = high - low
    right, left = neighbours(here, 1, width, first, last)
    slope = right - left
    d_right, d_left = neighbours(over_z, 1, width, first, last)
    down, up = rows_around(here, height)
    z_down, z_up = rows_around(over_z, height)
    s_down, s_up = rows_around(slope, height)
    total = k[0] * cut(high + low) + k[1] * cut(down + up) + k[2] * cut(right + left)
    total = total + k[3] * cut(z_down - z_up) + k[4] * cut(d_right - d_left)
    total = total + k[5] * cut(s_down - s_up)
    return total + k[6] * cut(here)


def pair_matrix(shape, long_axis, value):
    long = lax.broadcasted_iota(jnp.int32, shape, long_axis)
    short = lax.broadcasted_iota(jnp.int32, shape, 1 - long_axis)
    return jnp.where((long == 2 * short) | (long == 2 * short + 1), value, 0.0).astype(jnp.bfloat16)


def times(value, matrix):
    high = value.astype(jnp.bfloat16)
    low = (value - high.astype(F32)).astype(jnp.bfloat16)
    dot = functools.partial(jnp.dot, preferred_element_type=F32)
    return dot(high, matrix) + dot(low, matrix)


def loop(count, fn, unroll=1):
    def step(i, carry):
        fn(i)
        return carry

    lax.fori_loop(0, count, step, 0, unroll=unroll)


def kernel(
    nodes_hbm, coeffs_hbm, out,
    nodes, coeffs, kf, ab, bb, cb, v1, v2, v2p, kcp, rp, w0, wn, kb, rb, hb, ec, en, pairs, wide, narrow,
    halo_s, halo_r, shift_s, shift_r, k_s, k_r, r_s, r_r, hand_s, hand_r, e_s, e_r, f_s, f_r, in_s, kf_s, kf_r, known,
):
    t = lax.axis_index("tm")
    s = lax.axis_index("space")
    block = lax.div(t, BLOCK)
    place = lax.rem(t, BLOCK)
    base = block * BLOCK
    half = lax.div(s, 4)
    chunk = 4 * lax.rem(s, 2) + lax.div(place, 2)
    odd = lax.rem(lax.div(s, 2), 2)
    is_worker = (lax.rem(place, 2) == 0) & (lax.rem(chunk, 2) == jnp.where(half == 0, odd, 1 - odd))
    last_block = NT // BLOCK - 1
    strips = ROWS // STRIP

    def tell(sem, tm, sp):
        pl.semaphore_signal(sem, inc=1, device_id=(tm, sp), device_id_type=MESH)

    load_nodes = pltpu.make_async_copy(nodes_hbm, nodes, in_s.at[0])
    load_coeffs = pltpu.make_async_copy(coeffs_hbm, coeffs, in_s.at[1])
    load_nodes.start()
    load_coeffs.start()

    barrier = pltpu.get_barrier_semaphore()
    for n in range(1, SLABS):
        tell(barrier, t, lax.rem(s + n, SLABS))
    for n in range(1, BLOCK):
        tell(barrier, base + lax.rem(place + n, BLOCK), s)

    cross_up = (place == BLOCK - 1) & (t < NT - 1)
    cross_down = (place == 0) & (t > 0)

    @pl.when(cross_up)
    def _():
        tell(barrier, t + 1, s)

    @pl.when(cross_down)
    def _():
        tell(barrier, t - 1, s)

    @pl.when(is_worker)
    def _():
        for n in range(1, NT // BLOCK):
            tell(barrier, lax.rem(t + BLOCK * n, NT), s)

    for dj in (-1, 0, 1):
        j = chunk + dj

        @pl.when(is_worker & (block > 0) & (j >= 0) & (j < SLABS))
        def _(j=j):
            for z in (0, 1):
                to, at = worker(z, j)
                tell(barrier, base - BLOCK + to, at)

    for buf in (ab, bb, cb):
        buf[:, 0:RIM, :] = jnp.zeros((DEPTH + 2, RIM, COLS), F32)
        buf[:, RIM + ROWS :, :] = jnp.zeros((DEPTH + 2, RIM, COLS), F32)

    @pl.when(s == 0)
    def _():
        for buf in (ab, bb, cb):
            buf[0, RIM : RIM + ROWS, :] = jnp.zeros((ROWS, COLS), F32)

    @pl.when(s == SLABS - 1)
    def _():
        for buf in (ab, bb, cb):
            buf[DEPTH + 1, RIM : RIM + ROWS, :] = jnp.zeros((ROWS, COLS), F32)

    kcp[:, 0:RIM, :] = jnp.zeros((7, RIM, LANES), F32)
    kcp[:, RIM + HALF :, :] = jnp.zeros((7, RIM, LANES), F32)
    rp[:, 0:RIM, :] = jnp.zeros((DEPTH, RIM, LANES), F32)
    rp[:, RIM + HALF :, :] = jnp.zeros((DEPTH, RIM, LANES), F32)

    def combine_a(p, i):
        here = pl.ds(pl.multiple_of(i * STRIP, STRIP), STRIP)
        there = pl.ds(pl.multiple_of(RIM + i * STRIP, 8), STRIP)
        ab[p + 1, there, :] = A0 * nodes[0, 0, p, here, :] + A1 * nodes[0, 1, p, here, :] + A2 * nodes[0, 2, p, here, :]

    load_nodes.wait()
    loop(strips, lambda i: combine_a(0, i))
    loop(strips, lambda i: combine_a(3, i))
    load_coeffs.wait()

    expect = 14 + jnp.where(cross_up, 1, 0) + jnp.where(cross_down, 1, 0)
    hands = 6 - jnp.where(chunk == 0, 2, 0) - jnp.where(chunk == SLABS - 1, 2, 0)
    expect = expect + jnp.where(is_worker, last_block, 0) + jnp.where(is_worker & (block < last_block), hands, 0)
    pl.semaphore_wait(barrier, expect)

    inner = pl.ds(RIM, ROWS)

    def halo(buf, phase, upward):
        return pltpu.make_async_remote_copy(
            src_ref=buf.at[DEPTH if upward else 1, inner],
            dst_ref=buf.at[0 if upward else DEPTH + 1, inner],
            send_sem=halo_s.at[phase, int(upward)],
            recv_sem=halo_r.at[phase, int(upward)],
            device_id=(t, s + 1 if upward else s - 1),
            device_id_type=MESH,
        )

    def send_halo(buf, phase, upward):
        @pl.when(s < SLABS - 1 if upward else s > 0)
        def _():
            halo(buf, phase, upward).start()

    def take_halo(buf, phase, upward):
        @pl.when(s > 0 if upward else s < SLABS - 1)
        def _():
            halo(buf, phase, upward).wait_recv()

    send_halo(ab, 0, False)
    send_halo(ab, 0, True)
    for n in range(1, BLOCK):
        tell(known, base + lax.rem(place + n, BLOCK), s)

    narrow[...] = pair_matrix((COLS, LANES), 0, 0.25)
    wide[...] = pair_matrix((LANES, COLS), 1, 1.0)

    def restrict(p, across):
        pairs[p] = across
        return pairs[p, pl.ds(0, HALF, stride=2), :] + pairs[p, pl.ds(1, HALF, stride=2), :]

    def average(p, value):
        return restrict(p, times(value, narrow[...]))

    def prolong(p, value):
        pairs[p, pl.ds(0, HALF, stride=2), :] = value
        pairs[p, pl.ds(1, HALF, stride=2), :] = value
        return times(pairs[p], wide[...])

    def shift(src, dst, n, tm):
        return pltpu.make_async_remote_copy(
            src_ref=src, dst_ref=dst, send_sem=shift_s.at[n], recv_sem=shift_r.at[n],
            device_id=(tm, s), device_id_type=MESH,
        )

    send_w0 = shift(w0, wn, 0, t - 1)
    send_v2 = shift(v2, v2p, 1, t + 1)

    for p in range(DEPTH):
        w0[p] = average(p, nodes[0, 0, p])

    @pl.when(t > 0)
    def _():
        send_w0.start()

    @pl.when(t == NT - 1)
    def _():
        wn[...] = jnp.zeros_like(wn)

    def weights(p, i):
        here = pl.ds(pl.multiple_of(i * STRIP, STRIP), STRIP)
        k = [coeffs[m, p, here, :].astype(F32) for m in range(7)]
        for m in range(3):
            kf[m, p, here, :] = k[m]
            kf[3 + m, p, here, :] = 0.5 * k[3 + m]
        kf[6, p, here, :] = -(2.0 * (k[0] + k[1] + k[2]) + k[6])

    loop(DEPTH * strips, lambda n: weights(lax.div(n, strips), lax.rem(n, strips)))
    loop(strips, lambda i: combine_a(1, i))
    loop(strips, lambda i: combine_a(2, i))

    def force(buf, p, i):
        window = pl.ds(pl.multiple_of(i * STRIP, STRIP), STRIP + 2 * RIM)
        here = pl.ds(pl.multiple_of(i * STRIP, STRIP), STRIP)
        return stencil(
            buf[p, window, :], buf[p + 1, window, :], buf[p + 2, window, :],
            [kf[m, p, here, :] for m in range(7)], STRIP + 2 * RIM, COLS, RIM, STRIP,
        )

    def spots(i):
        return (
            pl.ds(pl.multiple_of(i * STRIP, STRIP), STRIP),
            pl.ds(pl.multiple_of(RIM + i * STRIP, 8), STRIP),
        )

    def first_node(p, i):
        here, there = spots(i)
        value = nodes[0, 0, p, here, :] + force(ab, p, i)
        v1[p, here, :] = value
        bb[p + 1, there, :] = (
            0.1 * value + B0 * nodes[0, 0, p, here, :] + (B1 - 0.1) * nodes[0, 1, p, here, :] + B2 * nodes[0, 2, p, here, :]
        )

    def last_node(p, i):
        here, there = spots(i)
        first = v1[p, here, :]
        value = first + force(bb, p, i)
        v2[p, here, :] = value
        cb[p + 1, there, :] = C0 * (nodes[0, 0, p, here, :] + value) + C1 * first

    def add_force(p, i):
        here, there = spots(i)
        out[0, 0, p, here, :] = nodes[0, 0, p, here, :] + force(cb, p, i)

    def planes(fn, which):
        for p in which:
            loop(strips, lambda i, p=p: fn(p, i))

    inside = slice(RIM, RIM + HALF)
    k = []
    for m in range(7):
        across = jnp.dot(coeffs[m, block], narrow[...], preferred_element_type=F32)
        k.append(restrict(m % DEPTH, across))
    kcp[0, inside, :] = 0.2 * k[0]
    for m in range(1, 5):
        kcp[m, inside, :] = 0.05 * k[m]
    kcp[5, inside, :] = 0.025 * k[5]
    kcp[6, inside, :] = 1.0 - (0.4 * k[0] + 0.1 * (k[1] + k[2]) + 0.2 * k[6])
    planes(first_node, (1, 2))
    pl.semaphore_wait(known, BLOCK - 1)

    window = pl.ds(pl.multiple_of(8 * place, 8), WIN)

    def send_k(z):
        to, at = worker(z, place)
        src, dst = kcp.at[:, window], kb.at[:, s - 2 * z, block]
        own = (to == place) & (at == s)
        needed = s >= 2 if z else s <= 5
        copy = pltpu.make_async_remote_copy(
            src_ref=src, dst_ref=dst, send_sem=k_s.at[z], recv_sem=k_r.at[0],
            device_id=(base + to, at), device_id_type=MESH,
        )
        return needed & own, needed & jnp.logical_not(own), copy, pltpu.make_async_copy(src, dst, k_r.at[0])

    def start(parts):
        own, other, copy, local = parts

        @pl.when(own)
        def _():
            local.start()

        @pl.when(other)
        def _():
            copy.start()

    def end(parts):
        @pl.when(parts[1])
        def _():
            parts[2].wait_send()

    for z in (0, 1):
        start(send_k(z))

    def pass_k(n):
        part = kb.at[:, :, block]
        return pltpu.make_async_remote_copy(
            src_ref=part, dst_ref=part, send_sem=kf_s.at[n - 1], recv_sem=kf_r.at[block],
            device_id=(lax.rem(t + BLOCK * n, NT), s), device_id_type=MESH,
        )

    take_halo(ab, 0, True)
    planes(first_node, (0,))
    send_halo(bb, 1, False)
    take_halo(ab, 0, False)
    planes(first_node, (3,))
    send_halo(bb, 1, True)
    planes(last_node, (1, 2))
    take_halo(bb, 1, True)
    planes(last_node, (0,))
    send_halo(cb, 2, False)
    take_halo(bb, 1, False)
    planes(last_node, (3,))
    send_halo(cb, 2, True)

    @pl.when(is_worker)
    def _():
        part = kb.at[:, :, block]
        pltpu.make_async_copy(part, part, k_r.at[0]).wait()
        for n in range(1, NT // BLOCK):
            pass_k(n).start()

    on_chip = lax.rem(place, 2) == 0

    @pl.when(on_chip)
    def _():
        send_v2.start()

    planes(add_force, (1, 2))
    take_halo(cb, 2, True)
    planes(add_force, (0,))
    take_halo(cb, 2, False)
    planes(add_force, (3,))

    @pl.when(t < NT - 1)
    def _():
        send_w0.wait_recv()

    for p in range(DEPTH):
        rp[p, RIM : RIM + HALF, :] = average(p, out[0, 0, p]) - wn[p]

    def send_r(z, j):
        to, at = worker(z, j)
        src = rp.at[:, pl.ds(pl.multiple_of(8 * j, 8), WIN)]
        dst = rb.at[place, pl.ds(DEPTH * s - 8 * z, DEPTH)]
        own = (to == place) & (at == s)
        needed = DEPTH * s + 3 >= 9 + place if z else DEPTH * s < 23 - place
        copy = pltpu.make_async_remote_copy(
            src_ref=src, dst_ref=dst, send_sem=r_s.at[z, j], recv_sem=r_r.at[place, s],
            device_id=(base + to, at), device_id_type=MESH,
        )
        return needed & own, needed & jnp.logical_not(own), copy, pltpu.make_async_copy(src, dst, r_r.at[place, s])

    for z in (0, 1):
        loop(SLABS, lambda j, z=z: start(send_r(z, j)))

    @pl.when(jnp.logical_not(on_chip))
    def _():
        for z in (0, 1):
            loop(SLABS, lambda j, z=z: end(send_r(z, j)))

        @pl.when(t < NT - 1)
        def _():
            send_v2.start()

    def early_start():
        @pl.when(t > 0)
        def _():
            send_v2.wait_recv()
            for p in range(DEPTH):
                out[0, 0, p] = v2p[p] + prolong(p, average(p, nodes[0, 0, p] - v2p[p]))

        @pl.when(t == 0)
        def _():
            out[0, 0] = nodes[0, 0]

    for p in range(DEPTH):
        gap = prolong(p, wn[p] - average(p, v2[p]))
        out[0, 1, p] = v1[p] + 0.5 * gap
        out[0, 2, p] = v2[p] + gap

    pl.when(jnp.logical_not(is_worker))(early_start)

    def hand(z, dj):
        count = 8 if z else 16
        source = 9 if z else 1 + 8 * half
        target = jnp.where(half == 0, 1, 17) if z else source
        to, at = worker(1 - half if z else half, chunk + dj)
        return pltpu.make_async_remote_copy(
            src_ref=hb.at[BLOCK, pl.ds(source, count), pl.ds(8, 8)],
            dst_ref=hb.at[0, pl.ds(target, count), pl.ds(8 - 8 * dj, 8)],
            send_sem=hand_s.at[z, dj + 1],
            recv_sem=hand_r.at[z, dj + 1],
            device_id=(base + BLOCK + to, at),
            device_id_type=MESH,
        )

    def spread(h, n):
        to = 4 * half + n
        src = hb.at[h + 1, pl.ds(1 + 8 * half + DEPTH * n, DEPTH), pl.ds(8, 8)]
        dst = en.at[:, pl.ds(pl.multiple_of(8 * chunk, 8), 8)]
        own = (h == place) & (to == s)
        copy = pltpu.make_async_remote_copy(
            src_ref=src, dst_ref=dst, send_sem=e_s.at[h, n], recv_sem=e_r.at[0],
            device_id=(base + h, to), device_id_type=MESH,
        )
        return own, jnp.logical_not(own), copy, pltpu.make_async_copy(src, dst, e_r.at[0])

    def start_spread(h):
        loop(4, lambda n: start(spread(h, n)))

    @pl.when(is_worker)
    def _():
        def clear(h):
            hb[h, 0] = jnp.zeros((WIN, LANES), F32)
            hb[h, DEEP + 1] = jnp.zeros((WIN, LANES), F32)

        loop(BLOCK + 1, clear)

        @pl.when(block == 0)
        def _():
            hb[0, 1 : DEEP + 1] = jnp.zeros((DEEP, WIN, LANES), F32)

        @pl.when((block > 0) & (chunk == 0))
        def _():
            hb[0, 1 : DEEP + 1, 0:8, :] = jnp.zeros((DEEP, 8, LANES), F32)

        @pl.when((block > 0) & (chunk == SLABS - 1))
        def _():
            hb[0, 1 : DEEP + 1, 16:24, :] = jnp.zeros((DEEP, 8, LANES), F32)

        for n in range(1, NT // BLOCK):
            other = lax.rem(block + n, NT // BLOCK)
            part = kb.at[:, :, other]
            pltpu.make_async_copy(part, part, kf_r.at[other]).wait()
        for dj in (-1, 0, 1):
            @pl.when((block > 0) & (chunk - dj >= 0) & (chunk - dj < SLABS))
            def _(dj=dj):
                hand(0, dj).wait_recv()
                hand(1, dj).wait_recv()

        lane = lax.broadcasted_iota(jnp.int32, (WIN, LANES), 1)
        first, last = lane == 0, lane == LANES - 1

        def slopes(v):
            right, left = neighbours(v, 1, LANES, first, last)
            down, up = rows_around(v, WIN)
            over_y = right - left
            s_down, s_up = rows_around(over_y, WIN)
            return v, over_y, down - up, right + left, down + up, s_down - s_up

        def advance(h):
            count = lax.div(26 - h, 4)
            slab0 = half * (SLABS - count)
            quad = slab0 - 2 * half
            start_plane = DEPTH * quad

            def arrived(i):
                part = rb.at[h, pl.ds(start_plane + DEPTH * i, DEPTH)]
                pltpu.make_async_copy(part, part, r_r.at[h, slab0 + i]).wait()

            loop(count, arrived)
            low, low_y, low_x = slopes(hb[h, start_plane])[:3]

            def group(i, carry):
                (low, low_y, low_x), here = carry
                for n in range(DEPTH):
                    p = start_plane + DEPTH * i + n
                    above = slopes(hb[h, p + 2])
                    v, v_y, v_x, around_y, around_x, v_xy = here
                    k = [kb[m, quad + i, n] for m in range(7)]
                    total = rb[h, p] + k[0] * (above[0] + low) + k[1] * around_x + k[2] * around_y
                    total = total + k[3] * (above[2] - low_x) + k[4] * (above[1] - low_y)
                    hb[h + 1, p + 1] = total + k[5] * v_xy + k[6] * v
                    low, low_y, low_x = v, v_y, v_x
                    here = above
                return (low, low_y, low_x), here

            lax.fori_loop(0, count, group, ((low, low_y, low_x), slopes(hb[h, start_plane + 1])))

            @pl.when(block == last_block)
            def _():
                start_spread(h)

        loop(BLOCK, advance)

        @pl.when(block < last_block)
        def _():
            for dj in (-1, 0, 1):
                j = chunk + dj

                @pl.when((j >= 0) & (j < SLABS))
                def _(dj=dj):
                    hand(0, dj).start()
                    hand(1, dj).start()

            loop(BLOCK, start_spread)

    pltpu.make_async_copy(en, en, e_r.at[0]).wait()
    forward = pltpu.make_async_remote_copy(
        src_ref=en, dst_ref=ec, send_sem=f_s.at[0], recv_sem=f_r.at[0], device_id=(t + 1, s), device_id_type=MESH
    )

    @pl.when(t < NT - 1)
    def _():
        forward.start()

    for p in range(DEPTH):
        gain = prolong(p, en[p])
        out[0, 2, p] += gain
        out[0, 1, p] += 0.5 * gain

    pl.when(is_worker)(early_start)

    @pl.when(t > 0)
    def _():
        forward.wait_recv()

        for p in range(DEPTH):
            gain = prolong(p, ec[p])
            out[0, 0, p] += gain
            out[0, 1, p] += 0.5 * gain

    for phase, buf in enumerate((ab, bb, cb)):

        @pl.when(s < SLABS - 1)
        def _(phase=phase, buf=buf):
            halo(buf, phase, True).wait_send()

        @pl.when(s > 0)
        def _(phase=phase, buf=buf):
            halo(buf, phase, False).wait_send()

    @pl.when(t > 0)
    def _():
        send_w0.wait_send()

    @pl.when(t < NT - 1)
    def _():
        send_v2.wait_send()
        forward.wait_send()

    for z in (0, 1):
        end(send_k(z))

        @pl.when(on_chip)
        def _(z=z):
            loop(SLABS, lambda j: end(send_r(z, j)))

    @pl.when(is_worker)
    def _():
        for n in range(1, NT // BLOCK):
            pass_k(n).wait_send()

        for dj in (-1, 0, 1):
            j = chunk + dj

            @pl.when((block < last_block) & (j >= 0) & (j < SLABS))
            def _(dj=dj):
                hand(0, dj).wait_send()
                hand(1, dj).wait_send()

        def end_spread(h):
            loop(4, lambda n: end(spread(h, n)))

        loop(BLOCK, end_spread)


def body(nodes, coefficients):
    dma = pltpu.SemaphoreType.DMA
    fine = (DEPTH, ROWS, COLS)
    rimmed = (DEPTH + 2, ROWS + 2 * RIM, COLS)
    coarse = (DEPTH, HALF, LANES)
    scratch = [
        (7,) + fine, rimmed, rimmed, rimmed, fine, fine, fine,
        (7, HALF + 2 * RIM, LANES), (DEPTH, HALF + 2 * RIM, LANES), coarse, coarse,
        (7, DEEP // DEPTH, DEPTH, WIN, LANES), (BLOCK, DEEP, WIN, LANES), (BLOCK + 1, DEEP + 2, WIN, LANES), coarse, coarse,
        (DEPTH, ROWS, LANES),
    ]
    sems = [(3, 2), (3, 2), (2,), (2,), (2,), (1,), (2, 8), (8, 8), (2, 3), (2, 3), (8, 4), (1,), (1,), (1,), (2,), (3,), (4,)]
    return pl.pallas_call(
        kernel,
        out_shape=jax.ShapeDtypeStruct(nodes.shape, F32),
        in_specs=[pl.BlockSpec(memory_space=pltpu.HBM)] * 2,
        out_specs=pl.BlockSpec(memory_space=pltpu.VMEM),
        scratch_shapes=[pltpu.VMEM(nodes.shape, F32), pltpu.VMEM(coefficients.shape, jnp.bfloat16)]
        + [pltpu.VMEM(shape, F32) for shape in scratch]
        + [pltpu.VMEM((LANES, COLS), jnp.bfloat16), pltpu.VMEM((COLS, LANES), jnp.bfloat16)]
        + [dma(shape) for shape in sems]
        + [pltpu.SemaphoreType.REGULAR],
        compiler_params=pltpu.CompilerParams(
            collective_id=0, has_side_effects=True, vmem_limit_bytes=48 * 1024 * 1024
        ),
        name="pfasst",
    )(nodes, coefficients)


def solution(mesh):
    return jax.shard_map(
        body,
        mesh=mesh,
        in_specs=(P("tm", None, "space", None, None), P(None, "space", None, None)),
        out_specs=P("tm", None, "space", None, None),
        check_vma=False,
    )
```

```python
import functools

import jax
import jax.numpy as jnp
from jax import lax
from jax.experimental import pallas as pl
from jax.experimental.pallas import tpu as pltpu
from jax.sharding import PartitionSpec as P

MESH = pl.DeviceIdType.MESH
F32 = jnp.float32

A0, A1, A2 = 0.2 * 5.0 / 24.0, 0.2 / 3.0, -0.2 / 24.0
B0, B1, B2 = -0.2 / 24.0, 0.2 / 3.0, 0.2 * 5.0 / 24.0
C0, C1 = 0.2 / 6.0, 0.2 * 2.0 / 3.0

DEPTH = 4
ROWS, COLS = 128, 256
HALF, LANES = 64, 128
SLABS = 8
BLOCK = 8
NT = 32
RIM = 8
STRIP = 32
FIRST = (0, 32, 64, 96, 128)
SECOND = (0, 24, 56, 88, 128)
THIRD = (0, 16, 48, 80, 128)
FOURTH = (0, 0, 32, 64, 128)
PIECES = 4
WIN = 24
DEEP = 24


def worker(half, j):
    odd = lax.rem(j, 2)
    return 2 * lax.rem(j, 4), 2 * jnp.where(half == 0, odd, 3 - odd) + lax.div(j, 4)


def neighbours(value, axis, size, mask_low, mask_high):
    ahead = pltpu.roll(value, size - 1, axis)
    behind = pltpu.roll(value, 1, axis)
    return jnp.where(mask_high, 0.0, ahead), jnp.where(mask_low, 0.0, behind)


def rows_around(value, size):
    return pltpu.roll(value, size - 1, 0), pltpu.roll(value, 1, 0)


def stencil(low, here, high, k, height, width, top, rows):
    lane = lax.broadcasted_iota(jnp.int32, (height, width), 1)
    first, last = lane == 0, lane == width - 1
    cut = lambda v: v[top : top + rows]
    over_z = high - low
    right, left = neighbours(here, 1, width, first, last)
    slope = right - left
    d_right, d_left = neighbours(over_z, 1, width, first, last)
    down, up = rows_around(here, height)
    z_down, z_up = rows_around(over_z, height)
    s_down, s_up = rows_around(slope, height)
    total = k[0] * cut(high + low) + k[1] * cut(down + up) + k[2] * cut(right + left)
    total = total + k[3] * cut(z_down - z_up) + k[4] * cut(d_right - d_left)
    total = total + k[5] * cut(s_down - s_up)
    return total + k[6] * cut(here)


def pair_matrix(shape, long_axis, value):
    long = lax.broadcasted_iota(jnp.int32, shape, long_axis)
    short = lax.broadcasted_iota(jnp.int32, shape, 1 - long_axis)
    return jnp.where((long == 2 * short) | (long == 2 * short + 1), value, 0.0).astype(jnp.bfloat16)


def times(value, matrix):
    high = value.astype(jnp.bfloat16)
    low = (value - high.astype(F32)).astype(jnp.bfloat16)
    dot = functools.partial(jnp.dot, preferred_element_type=F32)
    return dot(high, matrix) + dot(low, matrix)


def loop(count, fn, unroll=1):
    def step(i, carry):
        fn(i)
        return carry

    lax.fori_loop(0, count, step, 0, unroll=unroll)


def kernel(
    nodes_hbm, coeffs_hbm, out,
    nodes, coeffs, kf, ab, bb, cb, v1, v2, v2p, kcp, rp, w0, wn, kb, rb, hb, ec, en, pairs, wide, narrow,
    halo_s, halo_r, shift_s, shift_r, k_s, k_r, r_s, r_r, hand_s, hand_r, e_s, e_r, f_s, f_r, in_s, kf_s, kf_r, known,
):
    t = lax.axis_index("tm")
    s = lax.axis_index("space")
    block = lax.div(t, BLOCK)
    place = lax.rem(t, BLOCK)
    base = block * BLOCK
    half = lax.div(s, 4)
    chunk = 4 * lax.rem(s, 2) + lax.div(place, 2)
    odd = lax.rem(lax.div(s, 2), 2)
    is_worker = (lax.rem(place, 2) == 0) & (lax.rem(chunk, 2) == jnp.where(half == 0, odd, 1 - odd))
    last_block = NT // BLOCK - 1
    strips = ROWS // STRIP

    def tell(sem, tm, sp):
        pl.semaphore_signal(sem, inc=1, device_id=(tm, sp), device_id_type=MESH)

    load_nodes = pltpu.make_async_copy(nodes_hbm, nodes, in_s.at[0])
    load_coeffs = pltpu.make_async_copy(coeffs_hbm, coeffs, in_s.at[1])
    load_nodes.start()
    load_coeffs.start()

    barrier = pltpu.get_barrier_semaphore()
    for n in range(1, SLABS):
        tell(barrier, t, lax.rem(s + n, SLABS))
    for n in range(1, BLOCK):
        tell(barrier, base + lax.rem(place + n, BLOCK), s)

    cross_up = (place == BLOCK - 1) & (t < NT - 1)
    cross_down = (place == 0) & (t > 0)

    @pl.when(cross_up)
    def _():
        tell(barrier, t + 1, s)

    @pl.when(cross_down)
    def _():
        tell(barrier, t - 1, s)

    @pl.when(is_worker)
    def _():
        for n in range(1, NT // BLOCK):
            tell(barrier, lax.rem(t + BLOCK * n, NT), s)

    for dj in (-1, 0, 1):
        j = chunk + dj

        @pl.when(is_worker & (block > 0) & (j >= 0) & (j < SLABS))
        def _(j=j):
            for z in (0, 1):
                to, at = worker(z, j)
                tell(barrier, base - BLOCK + to, at)

    for buf in (ab, bb, cb):
        buf[:, 0:RIM, :] = jnp.zeros((DEPTH + 2, RIM, COLS), F32)
        buf[:, RIM + ROWS :, :] = jnp.zeros((DEPTH + 2, RIM, COLS), F32)

    @pl.when(s == 0)
    def _():
        for buf in (ab, bb, cb):
            buf[0, RIM : RIM + ROWS, :] = jnp.zeros((ROWS, COLS), F32)

    @pl.when(s == SLABS - 1)
    def _():
        for buf in (ab, bb, cb):
            buf[DEPTH + 1, RIM : RIM + ROWS, :] = jnp.zeros((ROWS, COLS), F32)

    kcp[:, 0:RIM, :] = jnp.zeros((7, RIM, LANES), F32)
    kcp[:, RIM + HALF :, :] = jnp.zeros((7, RIM, LANES), F32)
    rp[:, 0:RIM, :] = jnp.zeros((DEPTH, RIM, LANES), F32)
    rp[:, RIM + HALF :, :] = jnp.zeros((DEPTH, RIM, LANES), F32)

    def combine_a(p, i):
        here = pl.ds(pl.multiple_of(i * STRIP, STRIP), STRIP)
        there = pl.ds(pl.multiple_of(RIM + i * STRIP, 8), STRIP)
        ab[p + 1, there, :] = A0 * nodes[0, 0, p, here, :] + A1 * nodes[0, 1, p, here, :] + A2 * nodes[0, 2, p, here, :]

    load_nodes.wait()
    loop(strips, lambda i: combine_a(0, i))
    loop(strips, lambda i: combine_a(3, i))
    load_coeffs.wait()

    expect = 14 + jnp.where(cross_up, 1, 0) + jnp.where(cross_down, 1, 0)
    hands = 6 - jnp.where(chunk == 0, 2, 0) - jnp.where(chunk == SLABS - 1, 2, 0)
    expect = expect + jnp.where(is_worker, last_block, 0) + jnp.where(is_worker & (block < last_block), hands, 0)
    pl.semaphore_wait(barrier, expect)

    def halo(buf, phase, bounds, i, upward):
        rows = pl.ds(RIM + bounds[i], bounds[i + 1] - bounds[i])
        return pltpu.make_async_remote_copy(
            src_ref=buf.at[DEPTH if upward else 1, rows],
            dst_ref=buf.at[0 if upward else DEPTH + 1, rows],
            send_sem=halo_s.at[phase, int(upward), i],
            recv_sem=halo_r.at[phase, int(upward), i],
            device_id=(t, s + 1 if upward else s - 1),
            device_id_type=MESH,
        )

    def send_halo(buf, phase, bounds, i, upward):
        @pl.when(s < SLABS - 1 if upward else s > 0)
        def _():
            halo(buf, phase, bounds, i, upward).start()

    def take_halo(buf, phase, bounds, i, upward):
        @pl.when(s > 0 if upward else s < SLABS - 1)
        def _():
            halo(buf, phase, bounds, i, upward).wait_recv()

    for i in range(PIECES):
        send_halo(ab, 0, FIRST, i, False)
        send_halo(ab, 0, FIRST, i, True)
    for n in range(1, BLOCK):
        tell(known, base + lax.rem(place + n, BLOCK), s)

    narrow[...] = pair_matrix((COLS, LANES), 0, 0.25)
    wide[...] = pair_matrix((LANES, COLS), 1, 1.0)

    def restrict(p, across):
        pairs[p] = across
        return pairs[p, pl.ds(0, HALF, stride=2), :] + pairs[p, pl.ds(1, HALF, stride=2), :]

    def average(p, value):
        return restrict(p, times(value, narrow[...]))

    def prolong(p, value):
        pairs[p, pl.ds(0, HALF, stride=2), :] = value
        pairs[p, pl.ds(1, HALF, stride=2), :] = value
        return times(pairs[p], wide[...])

    def shift(src, dst, n, tm):
        return pltpu.make_async_remote_copy(
            src_ref=src, dst_ref=dst, send_sem=shift_s.at[n], recv_sem=shift_r.at[n],
            device_id=(tm, s), device_id_type=MESH,
        )

    send_w0 = shift(w0, wn, 0, t - 1)
    send_v2 = shift(v2, v2p, 1, t + 1)

    for p in range(DEPTH):
        w0[p] = average(p, nodes[0, 0, p])

    @pl.when(t > 0)
    def _():
        send_w0.start()

    @pl.when(t == NT - 1)
    def _():
        wn[...] = jnp.zeros_like(wn)

    def weights(p, i):
        here = pl.ds(pl.multiple_of(i * STRIP, STRIP), STRIP)
        k = [coeffs[m, p, here, :].astype(F32) for m in range(7)]
        for m in range(3):
            kf[m, p, here, :] = k[m]
            kf[3 + m, p, here, :] = 0.5 * k[3 + m]
        kf[6, p, here, :] = -(2.0 * (k[0] + k[1] + k[2]) + k[6])

    loop(DEPTH * strips, lambda n: weights(lax.div(n, strips), lax.rem(n, strips)))
    loop(strips, lambda i: combine_a(1, i))
    loop(strips, lambda i: combine_a(2, i))

    def force(buf, p, low, rows):
        window = slice(low, low + rows + 2 * RIM)
        here = slice(low, low + rows)
        return stencil(
            buf[p, window, :], buf[p + 1, window, :], buf[p + 2, window, :],
            [kf[m, p, here, :] for m in range(7)], rows + 2 * RIM, COLS, RIM, rows,
        )

    def first_node(p, low, rows):
        here = slice(low, low + rows)
        value = nodes[0, 0, p, here, :] + force(ab, p, low, rows)
        v1[p, here, :] = value
        bb[p + 1, RIM + low : RIM + low + rows, :] = (
            0.1 * value + B0 * nodes[0, 0, p, here, :] + (B1 - 0.1) * nodes[0, 1, p, here, :] + B2 * nodes[0, 2, p, here, :]
        )

    def last_node(p, low, rows):
        here = slice(low, low + rows)
        first = v1[p, here, :]
        value = first + force(bb, p, low, rows)
        v2[p, here, :] = value
        cb[p + 1, RIM + low : RIM + low + rows, :] = C0 * (nodes[0, 0, p, here, :] + value) + C1 * first

    def add_force(p, low, rows):
        here = slice(low, low + rows)
        out[0, 0, p, here, :] = nodes[0, 0, p, here, :] + force(cb, p, low, rows)

    def piece(fn, p, bounds, i):
        if bounds[i + 1] > bounds[i]:
            fn(p, bounds[i], bounds[i + 1] - bounds[i])

    inside = slice(RIM, RIM + HALF)
    k = []
    for m in range(7):
        across = jnp.dot(coeffs[m, block], narrow[...], preferred_element_type=F32)
        k.append(restrict(m % DEPTH, across))
    kcp[0, inside, :] = 0.2 * k[0]
    for m in range(1, 5):
        kcp[m, inside, :] = 0.05 * k[m]
    kcp[5, inside, :] = 0.025 * k[5]
    kcp[6, inside, :] = 1.0 - (0.4 * k[0] + 0.1 * (k[1] + k[2]) + 0.2 * k[6])
    for p in (1, 2):
        for i in range(PIECES):
            piece(first_node, p, FIRST, i)
    pl.semaphore_wait(known, BLOCK - 1)

    window = pl.ds(pl.multiple_of(8 * place, 8), WIN)

    def send_k(z):
        to, at = worker(z, place)
        src, dst = kcp.at[:, window], kb.at[:, s - 2 * z, block]
        own = (to == place) & (at == s)
        needed = s >= 2 if z else s <= 5
        copy = pltpu.make_async_remote_copy(
            src_ref=src, dst_ref=dst, send_sem=k_s.at[z], recv_sem=k_r.at[0],
            device_id=(base + to, at), device_id_type=MESH,
        )
        return needed & own, needed & jnp.logical_not(own), copy, pltpu.make_async_copy(src, dst, k_r.at[0])

    def start(parts):
        own, other, copy, local = parts

        @pl.when(own)
        def _():
            local.start()

        @pl.when(other)
        def _():
            copy.start()

    def end(parts):
        @pl.when(parts[1])
        def _():
            parts[2].wait_send()

    for z in (0, 1):
        start(send_k(z))

    def pass_k(n):
        part = kb.at[:, :, block]
        return pltpu.make_async_remote_copy(
            src_ref=part, dst_ref=part, send_sem=kf_s.at[n - 1], recv_sem=kf_r.at[block],
            device_id=(lax.rem(t + BLOCK * n, NT), s), device_id_type=MESH,
        )

    for i in range(PIECES):
        take_halo(ab, 0, FIRST, i, True)
        piece(first_node, 0, SECOND, i)
        send_halo(bb, 1, SECOND, i, False)
        take_halo(ab, 0, FIRST, i, False)
        piece(first_node, 3, SECOND, i)
        send_halo(bb, 1, SECOND, i, True)
        piece(last_node, 1, THIRD, i)
        piece(last_node, 2, THIRD, i)
    for i in range(PIECES):
        take_halo(bb, 1, SECOND, i, True)
        piece(last_node, 0, THIRD, i)
        send_halo(cb, 2, THIRD, i, False)
        take_halo(bb, 1, SECOND, i, False)
        piece(last_node, 3, THIRD, i)
        send_halo(cb, 2, THIRD, i, True)
        piece(add_force, 1, FOURTH, i)
        piece(add_force, 2, FOURTH, i)

    @pl.when(is_worker)
    def _():
        part = kb.at[:, :, block]
        pltpu.make_async_copy(part, part, k_r.at[0]).wait()
        for n in range(1, NT // BLOCK):
            pass_k(n).start()

    on_chip = lax.rem(place, 2) == 0

    @pl.when(on_chip)
    def _():
        send_v2.start()

    @pl.when(t < NT - 1)
    def _():
        send_w0.wait_recv()

    def right_side(p, low, rows):
        half_rows = rows // 2
        pairs[p, 0:rows] = times(out[0, 0, p, low : low + rows, :], narrow[...])
        both = pairs[p, pl.ds(0, half_rows, stride=2), :] + pairs[p, pl.ds(1, half_rows, stride=2), :]
        here = slice(low // 2, low // 2 + half_rows)
        rp[p, RIM + low // 2 : RIM + low // 2 + half_rows, :] = both - wn[p, here, :]

    def send_r(z, j):
        to, at = worker(z, j)
        src = rp.at[:, pl.ds(pl.multiple_of(8 * j, 8), WIN)]
        dst = rb.at[place, pl.ds(DEPTH * s - 8 * z, DEPTH)]
        own = (to == place) & (at == s)
        needed = DEPTH * s + 3 >= 9 + place if z else DEPTH * s < 23 - place
        copy = pltpu.make_async_remote_copy(
            src_ref=src, dst_ref=dst, send_sem=r_s.at[z, j], recv_sem=r_r.at[place, s],
            device_id=(base + to, at), device_id_type=MESH,
        )
        return needed & own, needed & jnp.logical_not(own), copy, pltpu.make_async_copy(src, dst, r_r.at[place, s])

    done = 0
    for i in range(PIECES):
        take_halo(cb, 2, THIRD, i, True)
        piece(add_force, 0, FOURTH, i)
        take_halo(cb, 2, THIRD, i, False)
        piece(add_force, 3, FOURTH, i)
        for p in range(DEPTH):
            piece(right_side, p, FOURTH, i)
        ready = SLABS if i == PIECES - 1 else max(FOURTH[i + 1] // 16 - 1, 0)
        if ready > done:
            for z in (0, 1):
                loop(ready - done, lambda j, z=z, done=done: start(send_r(z, done + j)))
        done = ready

    @pl.when(jnp.logical_not(on_chip))
    def _():
        for z in (0, 1):
            loop(SLABS, lambda j, z=z: end(send_r(z, j)))

        @pl.when(t < NT - 1)
        def _():
            send_v2.start()

    def early_start():
        @pl.when(t > 0)
        def _():
            send_v2.wait_recv()
            for p in range(DEPTH):
                out[0, 0, p] = v2p[p] + prolong(p, average(p, nodes[0, 0, p] - v2p[p]))

        @pl.when(t == 0)
        def _():
            out[0, 0] = nodes[0, 0]

    for p in range(DEPTH):
        gap = prolong(p, wn[p] - average(p, v2[p]))
        out[0, 1, p] = v1[p] + 0.5 * gap
        out[0, 2, p] = v2[p] + gap

    pl.when(jnp.logical_not(is_worker))(early_start)

    def hand(z, dj):
        count = 8 if z else 16
        source = 9 if z else 1 + 8 * half
        target = jnp.where(half == 0, 1, 17) if z else source
        to, at = worker(1 - half if z else half, chunk + dj)
        return pltpu.make_async_remote_copy(
            src_ref=hb.at[BLOCK, pl.ds(source, count), pl.ds(8, 8)],
            dst_ref=hb.at[0, pl.ds(target, count), pl.ds(8 - 8 * dj, 8)],
            send_sem=hand_s.at[z, dj + 1],
            recv_sem=hand_r.at[z, dj + 1],
            device_id=(base + BLOCK + to, at),
            device_id_type=MESH,
        )

    def spread(h, n):
        to = 4 * half + n
        src = hb.at[h + 1, pl.ds(1 + 8 * half + DEPTH * n, DEPTH), pl.ds(8, 8)]
        dst = en.at[:, pl.ds(pl.multiple_of(8 * chunk, 8), 8)]
        own = (h == place) & (to == s)
        copy = pltpu.make_async_remote_copy(
            src_ref=src, dst_ref=dst, send_sem=e_s.at[h, n], recv_sem=e_r.at[0],
            device_id=(base + h, to), device_id_type=MESH,
        )
        return own, jnp.logical_not(own), copy, pltpu.make_async_copy(src, dst, e_r.at[0])

    def start_spread(h):
        loop(4, lambda n: start(spread(h, n)))

    @pl.when(is_worker)
    def _():
        def clear(h):
            hb[h, 0] = jnp.zeros((WIN, LANES), F32)
            hb[h, DEEP + 1] = jnp.zeros((WIN, LANES), F32)

        loop(BLOCK + 1, clear)

        @pl.when(block == 0)
        def _():
            hb[0, 1 : DEEP + 1] = jnp.zeros((DEEP, WIN, LANES), F32)

        @pl.when((block > 0) & (chunk == 0))
        def _():
            hb[0, 1 : DEEP + 1, 0:8, :] = jnp.zeros((DEEP, 8, LANES), F32)

        @pl.when((block > 0) & (chunk == SLABS - 1))
        def _():
            hb[0, 1 : DEEP + 1, 16:24, :] = jnp.zeros((DEEP, 8, LANES), F32)

        for n in range(1, NT // BLOCK):
            other = lax.rem(block + n, NT // BLOCK)
            part = kb.at[:, :, other]
            pltpu.make_async_copy(part, part, kf_r.at[other]).wait()
        for dj in (-1, 0, 1):
            @pl.when((block > 0) & (chunk - dj >= 0) & (chunk - dj < SLABS))
            def _(dj=dj):
                hand(0, dj).wait_recv()
                hand(1, dj).wait_recv()

        lane = lax.broadcasted_iota(jnp.int32, (WIN, LANES), 1)
        first, last = lane == 0, lane == LANES - 1

        def slopes(v):
            right, left = neighbours(v, 1, LANES, first, last)
            down, up = rows_around(v, WIN)
            over_y = right - left
            s_down, s_up = rows_around(over_y, WIN)
            return v, over_y, down - up, right + left, down + up, s_down - s_up

        def advance(h):
            count = lax.div(26 - h, 4)
            slab0 = half * (SLABS - count)
            quad = slab0 - 2 * half
            start_plane = DEPTH * quad

            def arrived(i):
                part = rb.at[h, pl.ds(start_plane + DEPTH * i, DEPTH)]
                pltpu.make_async_copy(part, part, r_r.at[h, slab0 + i]).wait()

            loop(count, arrived)
            low, low_y, low_x = slopes(hb[h, start_plane])[:3]

            def group(i, carry, planes):
                (low, low_y, low_x), here = carry
                for n in range(planes):
                    p = start_plane + DEPTH * i + n
                    above = slopes(hb[h, p + 2])
                    v, v_y, v_x, around_y, around_x, v_xy = here
                    k = [kb[m, quad + i + n // DEPTH, n % DEPTH] for m in range(7)]
                    total = rb[h, p] + k[0] * (above[0] + low) + k[1] * around_x + k[2] * around_y
                    total = total + k[3] * (above[2] - low_x) + k[4] * (above[1] - low_y)
                    hb[h + 1, p + 1] = total + k[5] * v_xy + k[6] * v
                    low, low_y, low_x = v, v_y, v_x
                    here = above
                return (low, low_y, low_x), here

            for some in (6, 5, 4):

                @pl.when(count == some)
                def _(some=some):
                    group(0, ((low, low_y, low_x), slopes(hb[h, start_plane + 1])), DEPTH * some)

            @pl.when(block == last_block)
            def _():
                start_spread(h)

        loop(BLOCK, advance)

        @pl.when(block < last_block)
        def _():
            for dj in (-1, 0, 1):
                j = chunk + dj

                @pl.when((j >= 0) & (j < SLABS))
                def _(dj=dj):
                    hand(0, dj).start()
                    hand(1, dj).start()

            loop(BLOCK, start_spread)

    pltpu.make_async_copy(en, en, e_r.at[0]).wait()
    forward = pltpu.make_async_remote_copy(
        src_ref=en, dst_ref=ec, send_sem=f_s.at[0], recv_sem=f_r.at[0], device_id=(t + 1, s), device_id_type=MESH
    )

    @pl.when(t < NT - 1)
    def _():
        forward.start()

    for p in range(DEPTH):
        gain = prolong(p, en[p])
        out[0, 2, p] += gain
        out[0, 1, p] += 0.5 * gain

    pl.when(is_worker)(early_start)

    @pl.when(t > 0)
    def _():
        forward.wait_recv()

        for p in range(DEPTH):
            gain = prolong(p, ec[p])
            out[0, 0, p] += gain
            out[0, 1, p] += 0.5 * gain

    for phase, (buf, bounds) in enumerate(((ab, FIRST), (bb, SECOND), (cb, THIRD))):
        for i in range(PIECES):

            @pl.when(s < SLABS - 1)
            def _(phase=phase, buf=buf, bounds=bounds, i=i):
                halo(buf, phase, bounds, i, True).wait_send()

            @pl.when(s > 0)
            def _(phase=phase, buf=buf, bounds=bounds, i=i):
                halo(buf, phase, bounds, i, False).wait_send()

    @pl.when(t > 0)
    def _():
        send_w0.wait_send()

    @pl.when(t < NT - 1)
    def _():
        send_v2.wait_send()
        forward.wait_send()

    for z in (0, 1):
        end(send_k(z))

        @pl.when(on_chip)
        def _(z=z):
            loop(SLABS, lambda j: end(send_r(z, j)))

    @pl.when(is_worker)
    def _():
        for n in range(1, NT // BLOCK):
            pass_k(n).wait_send()

        for dj in (-1, 0, 1):
            j = chunk + dj

            @pl.when((block < last_block) & (j >= 0) & (j < SLABS))
            def _(dj=dj):
                hand(0, dj).wait_send()
                hand(1, dj).wait_send()

        def end_spread(h):
            loop(4, lambda n: end(spread(h, n)))

        loop(BLOCK, end_spread)


def body(nodes, coefficients):
    dma = pltpu.SemaphoreType.DMA
    fine = (DEPTH, ROWS, COLS)
    rimmed = (DEPTH + 2, ROWS + 2 * RIM, COLS)
    coarse = (DEPTH, HALF, LANES)
    scratch = [
        (7,) + fine, rimmed, rimmed, rimmed, fine, fine, fine,
        (7, HALF + 2 * RIM, LANES), (DEPTH, HALF + 2 * RIM, LANES), coarse, coarse,
        (7, DEEP // DEPTH, DEPTH, WIN, LANES), (BLOCK, DEEP, WIN, LANES), (BLOCK + 1, DEEP + 2, WIN, LANES), coarse, coarse,
        (DEPTH, ROWS, LANES),
    ]
    sems = [(3, 2, PIECES), (3, 2, PIECES), (2,), (2,), (2,), (1,), (2, 8), (8, 8), (2, 3), (2, 3), (8, 4), (1,), (1,), (1,), (2,), (3,), (4,)]
    return pl.pallas_call(
        kernel,
        out_shape=jax.ShapeDtypeStruct(nodes.shape, F32),
        in_specs=[pl.BlockSpec(memory_space=pltpu.HBM)] * 2,
        out_specs=pl.BlockSpec(memory_space=pltpu.VMEM),
        scratch_shapes=[pltpu.VMEM(nodes.shape, F32), pltpu.VMEM(coefficients.shape, jnp.bfloat16)]
        + [pltpu.VMEM(shape, F32) for shape in scratch]
        + [pltpu.VMEM((LANES, COLS), jnp.bfloat16), pltpu.VMEM((COLS, LANES), jnp.bfloat16)]
        + [dma(shape) for shape in sems]
        + [pltpu.SemaphoreType.REGULAR],
        compiler_params=pltpu.CompilerParams(
            collective_id=0, has_side_effects=True, vmem_limit_bytes=48 * 1024 * 1024
        ),
        name="pfasst",
    )(nodes, coefficients)


def solution(mesh):
    return jax.shard_map(
        body,
        mesh=mesh,
        in_specs=(P("tm", None, "space", None, None), P(None, "space", None, None)),
        out_specs=P("tm", None, "space", None, None),
        check_vma=False,
    )
```

```python
import functools

import jax
import jax.numpy as jnp
from jax import lax
from jax.experimental import pallas as pl
from jax.experimental.pallas import tpu as pltpu
from jax.sharding import PartitionSpec as P

MESH = pl.DeviceIdType.MESH
F32 = jnp.float32

A0, A1, A2 = 0.2 * 5.0 / 24.0, 0.2 / 3.0, -0.2 / 24.0
B0, B1, B2 = -0.2 / 24.0, 0.2 / 3.0, 0.2 * 5.0 / 24.0
C0, C1 = 0.2 / 6.0, 0.2 * 2.0 / 3.0

DEPTH = 4
ROWS, COLS = 128, 256
HALF, LANES = 64, 128
SLABS = 8
BLOCK = 8
NT = 32
RIM = 8
STRIP = 32
FIRST = (0, 32, 64, 96, 128)
SECOND = (0, 24, 56, 88, 128)
THIRD = (0, 16, 48, 80, 128)
FOURTH = (0, 0, 32, 64, 128)
PIECES = 4
WIN = 24
DEEP = 24


def worker(half, j):
    return 2 * lax.rem(j, 4), 2 * (1 + half) + lax.div(j, 4)


def neighbours(value, axis, size, mask_low, mask_high):
    ahead = pltpu.roll(value, size - 1, axis)
    behind = pltpu.roll(value, 1, axis)
    return jnp.where(mask_high, 0.0, ahead), jnp.where(mask_low, 0.0, behind)


def rows_around(value, size):
    return pltpu.roll(value, size - 1, 0), pltpu.roll(value, 1, 0)


def stencil(low, here, high, k, height, width, top, rows):
    lane = lax.broadcasted_iota(jnp.int32, (height, width), 1)
    first, last = lane == 0, lane == width - 1
    cut = lambda v: v[top : top + rows]
    over_z = high - low
    right, left = neighbours(here, 1, width, first, last)
    slope = right - left
    d_right, d_left = neighbours(over_z, 1, width, first, last)
    down, up = rows_around(here, height)
    z_down, z_up = rows_around(over_z, height)
    s_down, s_up = rows_around(slope, height)
    total = k[0] * cut(high + low) + k[1] * cut(down + up) + k[2] * cut(right + left)
    total = total + k[3] * cut(z_down - z_up) + k[4] * cut(d_right - d_left)
    total = total + k[5] * cut(s_down - s_up)
    return total + k[6] * cut(here)


def pair_matrix(shape, long_axis, value):
    long = lax.broadcasted_iota(jnp.int32, shape, long_axis)
    short = lax.broadcasted_iota(jnp.int32, shape, 1 - long_axis)
    return jnp.where((long == 2 * short) | (long == 2 * short + 1), value, 0.0).astype(jnp.bfloat16)


def times(value, matrix):
    high = value.astype(jnp.bfloat16)
    low = (value - high.astype(F32)).astype(jnp.bfloat16)
    dot = functools.partial(jnp.dot, preferred_element_type=F32)
    return dot(high, matrix) + dot(low, matrix)


def loop(count, fn, unroll=1):
    def step(i, carry):
        fn(i)
        return carry

    lax.fori_loop(0, count, step, 0, unroll=unroll)


def kernel(
    nodes_hbm, coeffs_hbm, out,
    nodes, coeffs, kf, ab, bb, cb, v1, v2, v2p, kcp, rp, w0, wn, kb, rb, hb, ec, en, pairs, wide, narrow,
    halo_s, halo_r, shift_s, shift_r, k_s, k_r, r_s, r_r, hand_s, hand_r, e_s, e_r, f_s, f_r, in_s, kf_s, kf_r, known,
):
    t = lax.axis_index("tm")
    s = lax.axis_index("space")
    block = lax.div(t, BLOCK)
    place = lax.rem(t, BLOCK)
    base = block * BLOCK
    half = lax.div(s, 4)
    chunk = 4 * lax.rem(s, 2) + lax.div(place, 2)
    is_worker = (lax.rem(place, 2) == 0) & (lax.div(s, 2) == 1 + half)
    last_block = NT // BLOCK - 1
    strips = ROWS // STRIP

    def tell(sem, tm, sp):
        pl.semaphore_signal(sem, inc=1, device_id=(tm, sp), device_id_type=MESH)

    load_nodes = pltpu.make_async_copy(nodes_hbm, nodes, in_s.at[0])
    load_coeffs = pltpu.make_async_copy(coeffs_hbm, coeffs, in_s.at[1])
    load_nodes.start()
    load_coeffs.start()

    barrier = pltpu.get_barrier_semaphore()
    for n in range(1, SLABS):
        tell(barrier, t, lax.rem(s + n, SLABS))
    for n in range(1, BLOCK):
        tell(barrier, base + lax.rem(place + n, BLOCK), s)

    cross_up = (place == BLOCK - 1) & (t < NT - 1)
    cross_down = (place == 0) & (t > 0)

    @pl.when(cross_up)
    def _():
        tell(barrier, t + 1, s)

    @pl.when(cross_down)
    def _():
        tell(barrier, t - 1, s)

    @pl.when(is_worker)
    def _():
        for n in range(1, NT // BLOCK):
            tell(barrier, lax.rem(t + BLOCK * n, NT), s)

    for dj in (-1, 0, 1):
        j = chunk + dj

        @pl.when(is_worker & (block > 0) & (j >= 0) & (j < SLABS))
        def _(j=j):
            for z in (0, 1):
                to, at = worker(z, j)
                tell(barrier, base - BLOCK + to, at)

    for buf in (ab, bb, cb):
        buf[:, 0:RIM, :] = jnp.zeros((DEPTH + 2, RIM, COLS), F32)
        buf[:, RIM + ROWS :, :] = jnp.zeros((DEPTH + 2, RIM, COLS), F32)

    @pl.when(s == 0)
    def _():
        for buf in (ab, bb, cb):
            buf[0, RIM : RIM + ROWS, :] = jnp.zeros((ROWS, COLS), F32)

    @pl.when(s == SLABS - 1)
    def _():
        for buf in (ab, bb, cb):
            buf[DEPTH + 1, RIM : RIM + ROWS, :] = jnp.zeros((ROWS, COLS), F32)

    kcp[:, 0:RIM, :] = jnp.zeros((7, RIM, LANES), F32)
    kcp[:, RIM + HALF :, :] = jnp.zeros((7, RIM, LANES), F32)
    rp[:, 0:RIM, :] = jnp.zeros((DEPTH, RIM, LANES), F32)
    rp[:, RIM + HALF :, :] = jnp.zeros((DEPTH, RIM, LANES), F32)

    def combine_a(p, i):
        here = pl.ds(pl.multiple_of(i * STRIP, STRIP), STRIP)
        there = pl.ds(pl.multiple_of(RIM + i * STRIP, 8), STRIP)
        ab[p + 1, there, :] = A0 * nodes[0, 0, p, here, :] + A1 * nodes[0, 1, p, here, :] + A2 * nodes[0, 2, p, here, :]

    load_nodes.wait()
    loop(strips, lambda i: combine_a(0, i))
    loop(strips, lambda i: combine_a(3, i))
    load_coeffs.wait()

    expect = 14 + jnp.where(cross_up, 1, 0) + jnp.where(cross_down, 1, 0)
    hands = 6 - jnp.where(chunk == 0, 2, 0) - jnp.where(chunk == SLABS - 1, 2, 0)
    expect = expect + jnp.where(is_worker, last_block, 0) + jnp.where(is_worker & (block < last_block), hands, 0)
    pl.semaphore_wait(barrier, expect)

    def halo(buf, phase, bounds, i, upward):
        rows = pl.ds(RIM + bounds[i], bounds[i + 1] - bounds[i])
        return pltpu.make_async_remote_copy(
            src_ref=buf.at[DEPTH if upward else 1, rows],
            dst_ref=buf.at[0 if upward else DEPTH + 1, rows],
            send_sem=halo_s.at[phase, int(upward), i],
            recv_sem=halo_r.at[phase, int(upward), i],
            device_id=(t, s + 1 if upward else s - 1),
            device_id_type=MESH,
        )

    def send_halo(buf, phase, bounds, i, upward):
        @pl.when(s < SLABS - 1 if upward else s > 0)
        def _():
            halo(buf, phase, bounds, i, upward).start()

    def take_halo(buf, phase, bounds, i, upward):
        @pl.when(s > 0 if upward else s < SLABS - 1)
        def _():
            halo(buf, phase, bounds, i, upward).wait_recv()

    for i in range(PIECES):
        send_halo(ab, 0, FIRST, i, False)
        send_halo(ab, 0, FIRST, i, True)
    for n in range(1, BLOCK):
        tell(known, base + lax.rem(place + n, BLOCK), s)

    narrow[...] = pair_matrix((COLS, LANES), 0, 0.25)
    wide[...] = pair_matrix((LANES, COLS), 1, 1.0)

    def restrict(p, across):
        pairs[p] = across
        return pairs[p, pl.ds(0, HALF, stride=2), :] + pairs[p, pl.ds(1, HALF, stride=2), :]

    def average(p, value):
        return restrict(p, times(value, narrow[...]))

    def prolong(p, value):
        pairs[p, pl.ds(0, HALF, stride=2), :] = value
        pairs[p, pl.ds(1, HALF, stride=2), :] = value
        return times(pairs[p], wide[...])

    def shift(src, dst, n, tm):
        return pltpu.make_async_remote_copy(
            src_ref=src, dst_ref=dst, send_sem=shift_s.at[n], recv_sem=shift_r.at[n],
            device_id=(tm, s), device_id_type=MESH,
        )

    send_w0 = shift(w0, wn, 0, t - 1)
    send_v2 = shift(v2, v2p, 1, t + 1)

    for p in range(DEPTH):
        w0[p] = average(p, nodes[0, 0, p])

    @pl.when(t > 0)
    def _():
        send_w0.start()

    @pl.when(t == NT - 1)
    def _():
        wn[...] = jnp.zeros_like(wn)

    def weights(p, i):
        here = pl.ds(pl.multiple_of(i * STRIP, STRIP), STRIP)
        k = [coeffs[m, p, here, :].astype(F32) for m in range(7)]
        for m in range(3):
            kf[m, p, here, :] = k[m]
            kf[3 + m, p, here, :] = 0.5 * k[3 + m]
        kf[6, p, here, :] = -(2.0 * (k[0] + k[1] + k[2]) + k[6])

    loop(DEPTH * strips, lambda n: weights(lax.div(n, strips), lax.rem(n, strips)))
    loop(strips, lambda i: combine_a(1, i))
    loop(strips, lambda i: combine_a(2, i))

    def force(buf, p, low, rows):
        window = slice(low, low + rows + 2 * RIM)
        here = slice(low, low + rows)
        return stencil(
            buf[p, window, :], buf[p + 1, window, :], buf[p + 2, window, :],
            [kf[m, p, here, :] for m in range(7)], rows + 2 * RIM, COLS, RIM, rows,
        )

    def first_node(p, low, rows):
        here = slice(low, low + rows)
        value = nodes[0, 0, p, here, :] + force(ab, p, low, rows)
        v1[p, here, :] = value
        bb[p + 1, RIM + low : RIM + low + rows, :] = (
            0.1 * value + B0 * nodes[0, 0, p, here, :] + (B1 - 0.1) * nodes[0, 1, p, here, :] + B2 * nodes[0, 2, p, here, :]
        )

    def last_node(p, low, rows):
        here = slice(low, low + rows)
        first = v1[p, here, :]
        value = first + force(bb, p, low, rows)
        v2[p, here, :] = value
        cb[p + 1, RIM + low : RIM + low + rows, :] = C0 * (nodes[0, 0, p, here, :] + value) + C1 * first

    def add_force(p, low, rows):
        here = slice(low, low + rows)
        out[0, 0, p, here, :] = nodes[0, 0, p, here, :] + force(cb, p, low, rows)

    def piece(fn, p, bounds, i):
        if bounds[i + 1] > bounds[i]:
            fn(p, bounds[i], bounds[i + 1] - bounds[i])

    inside = slice(RIM, RIM + HALF)
    k = []
    for m in range(7):
        across = jnp.dot(coeffs[m, block], narrow[...], preferred_element_type=F32)
        k.append(restrict(m % DEPTH, across))
    kcp[0, inside, :] = 0.2 * k[0]
    for m in range(1, 5):
        kcp[m, inside, :] = 0.05 * k[m]
    kcp[5, inside, :] = 0.025 * k[5]
    kcp[6, inside, :] = 1.0 - (0.4 * k[0] + 0.1 * (k[1] + k[2]) + 0.2 * k[6])
    for p in (1, 2):
        for i in range(PIECES):
            piece(first_node, p, FIRST, i)
    pl.semaphore_wait(known, BLOCK - 1)

    window = pl.ds(pl.multiple_of(8 * place, 8), WIN)

    def send_k(z):
        to, at = worker(z, place)
        src, dst = kcp.at[:, window], kb.at[:, s - 2 * z, block]
        own = (to == place) & (at == s)
        needed = s >= 2 if z else s <= 5
        copy = pltpu.make_async_remote_copy(
            src_ref=src, dst_ref=dst, send_sem=k_s.at[z], recv_sem=k_r.at[0],
            device_id=(base + to, at), device_id_type=MESH,
        )
        return needed & own, needed & jnp.logical_not(own), copy, pltpu.make_async_copy(src, dst, k_r.at[0])

    def start(parts):
        own, other, copy, local = parts

        @pl.when(own)
        def _():
            local.start()

        @pl.when(other)
        def _():
            copy.start()

    def end(parts):
        @pl.when(parts[1])
        def _():
            parts[2].wait_send()

    for z in (0, 1):
        start(send_k(z))

    def pass_k(n):
        part = kb.at[:, :, block]
        return pltpu.make_async_remote_copy(
            src_ref=part, dst_ref=part, send_sem=kf_s.at[n - 1], recv_sem=kf_r.at[block],
            device_id=(lax.rem(t + BLOCK * n, NT), s), device_id_type=MESH,
        )

    for i in range(PIECES):
        take_halo(ab, 0, FIRST, i, True)
        piece(first_node, 0, SECOND, i)
        send_halo(bb, 1, SECOND, i, False)
        take_halo(ab, 0, FIRST, i, False)
        piece(first_node, 3, SECOND, i)
        send_halo(bb, 1, SECOND, i, True)
        piece(last_node, 1, THIRD, i)
        piece(last_node, 2, THIRD, i)
    for i in range(PIECES):
        take_halo(bb, 1, SECOND, i, True)
        piece(last_node, 0, THIRD, i)
        send_halo(cb, 2, THIRD, i, False)
        take_halo(bb, 1, SECOND, i, False)
        piece(last_node, 3, THIRD, i)
        send_halo(cb, 2, THIRD, i, True)
        piece(add_force, 1, FOURTH, i)
        piece(add_force, 2, FOURTH, i)

    @pl.when(is_worker)
    def _():
        part = kb.at[:, :, block]
        pltpu.make_async_copy(part, part, k_r.at[0]).wait()
        for n in range(1, NT // BLOCK):

            @pl.when(block == NT // BLOCK - n)
            def _(n=n):
                pass_k(n).start()

    on_chip = lax.rem(place, 2) == 0

    @pl.when(on_chip)
    def _():
        send_v2.start()

    @pl.when(t < NT - 1)
    def _():
        send_w0.wait_recv()

    def right_side(p, low, rows):
        half_rows = rows // 2
        pairs[p, 0:rows] = times(out[0, 0, p, low : low + rows, :], narrow[...])
        both = pairs[p, pl.ds(0, half_rows, stride=2), :] + pairs[p, pl.ds(1, half_rows, stride=2), :]
        here = slice(low // 2, low // 2 + half_rows)
        rp[p, RIM + low // 2 : RIM + low // 2 + half_rows, :] = both - wn[p, here, :]

    def send_r(z, j):
        to, at = worker(z, j)
        src = rp.at[:, pl.ds(pl.multiple_of(8 * j, 8), WIN)]
        dst = rb.at[place, pl.ds(DEPTH * s - 8 * z, DEPTH)]
        own = (to == place) & (at == s)
        needed = DEPTH * s + 3 >= 9 + place if z else DEPTH * s < 23 - place
        copy = pltpu.make_async_remote_copy(
            src_ref=src, dst_ref=dst, send_sem=r_s.at[z, j], recv_sem=r_r.at[place, s],
            device_id=(base + to, at), device_id_type=MESH,
        )
        return needed & own, needed & jnp.logical_not(own), copy, pltpu.make_async_copy(src, dst, r_r.at[place, s])

    done = 0
    for i in range(PIECES):
        take_halo(cb, 2, THIRD, i, True)
        piece(add_force, 0, FOURTH, i)
        take_halo(cb, 2, THIRD, i, False)
        piece(add_force, 3, FOURTH, i)
        for p in range(DEPTH):
            piece(right_side, p, FOURTH, i)
        ready = SLABS if i == PIECES - 1 else max(FOURTH[i + 1] // 16 - 1, 0)
        if ready > done:
            for z in (0, 1):
                loop(ready - done, lambda j, z=z, done=done: start(send_r(z, done + j)))
        done = ready

    @pl.when(is_worker)
    def _():
        for n in range(1, NT // BLOCK):

            @pl.when(block != NT // BLOCK - n)
            def _(n=n):
                pass_k(n).start()

    @pl.when(jnp.logical_not(on_chip))
    def _():
        for z in (0, 1):
            loop(SLABS, lambda j, z=z: end(send_r(z, j)))

        @pl.when(t < NT - 1)
        def _():
            send_v2.start()

    def early_start():
        @pl.when(t > 0)
        def _():
            send_v2.wait_recv()
            for p in range(DEPTH):
                out[0, 0, p] = v2p[p] + prolong(p, average(p, nodes[0, 0, p] - v2p[p]))

        @pl.when(t == 0)
        def _():
            out[0, 0] = nodes[0, 0]

    for p in range(DEPTH):
        gap = prolong(p, wn[p] - average(p, v2[p]))
        out[0, 1, p] = v1[p] + 0.5 * gap
        out[0, 2, p] = v2[p] + gap

    pl.when(jnp.logical_not(is_worker))(early_start)

    def hand(z, dj):
        count = 8 if z else 16
        source = 9 if z else 1 + 8 * half
        target = jnp.where(half == 0, 1, 17) if z else source
        to, at = worker(1 - half if z else half, chunk + dj)
        return pltpu.make_async_remote_copy(
            src_ref=hb.at[BLOCK, pl.ds(source, count), pl.ds(8, 8)],
            dst_ref=hb.at[0, pl.ds(target, count), pl.ds(8 - 8 * dj, 8)],
            send_sem=hand_s.at[z, dj + 1],
            recv_sem=hand_r.at[z, dj + 1],
            device_id=(base + BLOCK + to, at),
            device_id_type=MESH,
        )

    def spread(h, n):
        to = 4 * half + n
        src = hb.at[h + 1, pl.ds(1 + 8 * half + DEPTH * n, DEPTH), pl.ds(8, 8)]
        dst = en.at[:, pl.ds(pl.multiple_of(8 * chunk, 8), 8)]
        own = (h == place) & (to == s)
        copy = pltpu.make_async_remote_copy(
            src_ref=src, dst_ref=dst, send_sem=e_s.at[h, n], recv_sem=e_r.at[0],
            device_id=(base + h, to), device_id_type=MESH,
        )
        return own, jnp.logical_not(own), copy, pltpu.make_async_copy(src, dst, e_r.at[0])

    def start_spread(h):
        loop(4, lambda n: start(spread(h, n)))

    @pl.when(is_worker)
    def _():
        def clear(h):
            hb[h, 0] = jnp.zeros((WIN, LANES), F32)
            hb[h, DEEP + 1] = jnp.zeros((WIN, LANES), F32)

        loop(BLOCK + 1, clear)

        @pl.when(block == 0)
        def _():
            hb[0, 1 : DEEP + 1] = jnp.zeros((DEEP, WIN, LANES), F32)

        @pl.when((block > 0) & (chunk == 0))
        def _():
            hb[0, 1 : DEEP + 1, 0:8, :] = jnp.zeros((DEEP, 8, LANES), F32)

        @pl.when((block > 0) & (chunk == SLABS - 1))
        def _():
            hb[0, 1 : DEEP + 1, 16:24, :] = jnp.zeros((DEEP, 8, LANES), F32)

        for n in range(1, NT // BLOCK):
            other = lax.rem(block + n, NT // BLOCK)
            part = kb.at[:, :, other]
            pltpu.make_async_copy(part, part, kf_r.at[other]).wait()
        for dj in (-1, 0, 1):
            @pl.when((block > 0) & (chunk - dj >= 0) & (chunk - dj < SLABS))
            def _(dj=dj):
                hand(0, dj).wait_recv()
                hand(1, dj).wait_recv()

        lane = lax.broadcasted_iota(jnp.int32, (WIN, LANES), 1)
        first, last = lane == 0, lane == LANES - 1

        def slopes(v):
            right, left = neighbours(v, 1, LANES, first, last)
            down, up = rows_around(v, WIN)
            over_y = right - left
            s_down, s_up = rows_around(over_y, WIN)
            return v, over_y, down - up, right + left, down + up, s_down - s_up

        def advance(h):
            count = lax.div(26 - h, 4)
            slab0 = half * (SLABS - count)
            quad = slab0 - 2 * half
            start_plane = DEPTH * quad

            def arrived(i):
                part = rb.at[h, pl.ds(start_plane + DEPTH * i, DEPTH)]
                pltpu.make_async_copy(part, part, r_r.at[h, slab0 + i]).wait()

            loop(count, arrived)
            low, low_y, low_x = slopes(hb[h, start_plane])[:3]

            def group(i, carry, planes):
                rows = slice(8, 16) if planes == 4 * DEPTH else slice(0, WIN)
                (low, low_y, low_x), here = carry
                for n in range(planes):
                    p = start_plane + DEPTH * i + n
                    above = slopes(hb[h, p + 2])
                    v, v_y, v_x, around_y, around_x, v_xy = here
                    k = [kb[m, quad + i + n // DEPTH, n % DEPTH, rows, :] for m in range(7)]
                    cut = lambda a: a[rows]
                    total = rb[h, p, rows, :] + k[0] * cut(above[0] + low) + k[1] * cut(around_x) + k[2] * cut(around_y)
                    total = total + k[3] * cut(above[2] - low_x) + k[4] * cut(above[1] - low_y)
                    hb[h + 1, p + 1, rows, :] = total + k[5] * cut(v_xy) + k[6] * cut(v)
                    low, low_y, low_x = v, v_y, v_x
                    here = above
                return (low, low_y, low_x), here

            for some in (6, 5, 4):

                @pl.when(count == some)
                def _(some=some):
                    group(0, ((low, low_y, low_x), slopes(hb[h, start_plane + 1])), DEPTH * some)

            @pl.when(block == last_block)
            def _():
                start_spread(h)

        loop(BLOCK, advance)

        @pl.when(block < last_block)
        def _():
            for z, dj in ((1, -1), (1, 1), (0, -1), (0, 1), (1, 0), (0, 0)):
                j = chunk + dj

                @pl.when((j >= 0) & (j < SLABS))
                def _(z=z, dj=dj):
                    hand(z, dj).start()

            loop(BLOCK, start_spread)

    pltpu.make_async_copy(en, en, e_r.at[0]).wait()
    forward = pltpu.make_async_remote_copy(
        src_ref=en, dst_ref=ec, send_sem=f_s.at[0], recv_sem=f_r.at[0], device_id=(t + 1, s), device_id_type=MESH
    )

    @pl.when(t < NT - 1)
    def _():
        forward.start()

    for p in range(DEPTH):
        gain = prolong(p, en[p])
        out[0, 2, p] += gain
        out[0, 1, p] += 0.5 * gain

    pl.when(is_worker)(early_start)

    @pl.when(t > 0)
    def _():
        forward.wait_recv()

        for p in range(DEPTH):
            gain = prolong(p, ec[p])
            out[0, 0, p] += gain
            out[0, 1, p] += 0.5 * gain

    for phase, (buf, bounds) in enumerate(((ab, FIRST), (bb, SECOND), (cb, THIRD))):
        for i in range(PIECES):

            @pl.when(s < SLABS - 1)
            def _(phase=phase, buf=buf, bounds=bounds, i=i):
                halo(buf, phase, bounds, i, True).wait_send()

            @pl.when(s > 0)
            def _(phase=phase, buf=buf, bounds=bounds, i=i):
                halo(buf, phase, bounds, i, False).wait_send()

    @pl.when(t > 0)
    def _():
        send_w0.wait_send()

    @pl.when(t < NT - 1)
    def _():
        send_v2.wait_send()
        forward.wait_send()

    for z in (0, 1):
        end(send_k(z))

        @pl.when(on_chip)
        def _(z=z):
            loop(SLABS, lambda j: end(send_r(z, j)))

    @pl.when(is_worker)
    def _():
        for n in range(1, NT // BLOCK):
            pass_k(n).wait_send()

        for dj in (-1, 0, 1):
            j = chunk + dj

            @pl.when((block < last_block) & (j >= 0) & (j < SLABS))
            def _(dj=dj):
                hand(0, dj).wait_send()
                hand(1, dj).wait_send()

        def end_spread(h):
            loop(4, lambda n: end(spread(h, n)))

        loop(BLOCK, end_spread)


def body(nodes, coefficients):
    dma = pltpu.SemaphoreType.DMA
    fine = (DEPTH, ROWS, COLS)
    rimmed = (DEPTH + 2, ROWS + 2 * RIM, COLS)
    coarse = (DEPTH, HALF, LANES)
    scratch = [
        (7,) + fine, rimmed, rimmed, rimmed, fine, fine, fine,
        (7, HALF + 2 * RIM, LANES), (DEPTH, HALF + 2 * RIM, LANES), coarse, coarse,
        (7, DEEP // DEPTH, DEPTH, WIN, LANES), (BLOCK, DEEP, WIN, LANES), (BLOCK + 1, DEEP + 2, WIN, LANES), coarse, coarse,
        (DEPTH, ROWS, LANES),
    ]
    sems = [(3, 2, PIECES), (3, 2, PIECES), (2,), (2,), (2,), (1,), (2, 8), (8, 8), (2, 3), (2, 3), (8, 4), (1,), (1,), (1,), (2,), (3,), (4,)]
    return pl.pallas_call(
        kernel,
        out_shape=jax.ShapeDtypeStruct(nodes.shape, F32),
        in_specs=[pl.BlockSpec(memory_space=pltpu.HBM)] * 2,
        out_specs=pl.BlockSpec(memory_space=pltpu.VMEM),
        scratch_shapes=[pltpu.VMEM(nodes.shape, F32), pltpu.VMEM(coefficients.shape, jnp.bfloat16)]
        + [pltpu.VMEM(shape, F32) for shape in scratch]
        + [pltpu.VMEM((LANES, COLS), jnp.bfloat16), pltpu.VMEM((COLS, LANES), jnp.bfloat16)]
        + [dma(shape) for shape in sems]
        + [pltpu.SemaphoreType.REGULAR],
        compiler_params=pltpu.CompilerParams(
            collective_id=0, has_side_effects=True, vmem_limit_bytes=48 * 1024 * 1024
        ),
        name="pfasst",
    )(nodes, coefficients)


def solution(mesh):
    return jax.shard_map(
        body,
        mesh=mesh,
        in_specs=(P("tm", None, "space", None, None), P(None, "space", None, None)),
        out_specs=P("tm", None, "space", None, None),
        check_vma=False,
    )
```

```python
import functools

import jax
import jax.numpy as jnp
from jax import lax
from jax.experimental import pallas as pl
from jax.experimental.pallas import tpu as pltpu
from jax.sharding import PartitionSpec as P

MESH = pl.DeviceIdType.MESH
F32 = jnp.float32

A0, A1, A2 = 0.2 * 5.0 / 24.0, 0.2 / 3.0, -0.2 / 24.0
B0, B1, B2 = -0.2 / 24.0, 0.2 / 3.0, 0.2 * 5.0 / 24.0
C0, C1 = 0.2 / 6.0, 0.2 * 2.0 / 3.0

DEPTH = 4
ROWS, COLS = 128, 256
HALF, LANES = 64, 128
SLABS = 8
BLOCK = 8
NT = 32
RIM = 8
STRIP = 32
FIRST = (0, 32, 64, 96, 128)
SECOND = (0, 24, 56, 88, 128)
THIRD = (0, 16, 48, 80, 128)
FOURTH = (0, 0, 32, 64, 128)
PIECES = 4
WIN = 24
DEEP = 24


def worker(half, j):
    return 2 * lax.rem(j, 4), 2 * (1 + half) + lax.div(j, 4)


def neighbours(value, axis, size, mask_low, mask_high):
    ahead = pltpu.roll(value, size - 1, axis)
    behind = pltpu.roll(value, 1, axis)
    return jnp.where(mask_high, 0.0, ahead), jnp.where(mask_low, 0.0, behind)


def rows_around(value, size):
    return pltpu.roll(value, size - 1, 0), pltpu.roll(value, 1, 0)


def stencil(low, here, high, k, height, width, top, rows):
    lane = lax.broadcasted_iota(jnp.int32, (height, width), 1)
    first, last = lane == 0, lane == width - 1
    cut = lambda v: v[top : top + rows]
    over_z = high - low
    right, left = neighbours(here, 1, width, first, last)
    slope = right - left
    d_right, d_left = neighbours(over_z, 1, width, first, last)
    down, up = rows_around(here, height)
    z_down, z_up = rows_around(over_z, height)
    s_down, s_up = rows_around(slope, height)
    total = k[0] * cut(high + low) + k[1] * cut(down + up) + k[2] * cut(right + left)
    total = total + k[3] * cut(z_down - z_up) + k[4] * cut(d_right - d_left)
    total = total + k[5] * cut(s_down - s_up)
    return total + k[6] * cut(here)


def pair_matrix(shape, long_axis, value):
    long = lax.broadcasted_iota(jnp.int32, shape, long_axis)
    short = lax.broadcasted_iota(jnp.int32, shape, 1 - long_axis)
    return jnp.where((long == 2 * short) | (long == 2 * short + 1), value, 0.0).astype(jnp.bfloat16)


def times(value, matrix):
    high = value.astype(jnp.bfloat16)
    low = (value - high.astype(F32)).astype(jnp.bfloat16)
    dot = functools.partial(jnp.dot, preferred_element_type=F32)
    return dot(high, matrix) + dot(low, matrix)


def loop(count, fn, unroll=1):
    def step(i, carry):
        fn(i)
        return carry

    lax.fori_loop(0, count, step, 0, unroll=unroll)


def kernel(
    nodes_hbm, coeffs_hbm, out,
    nodes, coeffs, kf, ab, bb, cb, v1, v2, v2p, kcp, rp, w0, wn, kb, rb, hb, ec, en, pairs, wide, narrow,
    halo_s, halo_r, shift_s, shift_r, k_s, k_r, r_s, r_r, hand_s, hand_r, e_s, e_r, f_s, f_r, in_s, kf_s, kf_r, known,
):
    t = lax.axis_index("tm")
    s = lax.axis_index("space")
    block = lax.div(t, BLOCK)
    place = lax.rem(t, BLOCK)
    base = block * BLOCK
    half = lax.div(s, 4)
    chunk = 4 * lax.rem(s, 2) + lax.div(place, 2)
    is_worker = (lax.rem(place, 2) == 0) & (lax.div(s, 2) == 1 + half)
    last_block = NT // BLOCK - 1
    strips = ROWS // STRIP

    def tell(sem, tm, sp):
        pl.semaphore_signal(sem, inc=1, device_id=(tm, sp), device_id_type=MESH)

    load_nodes = pltpu.make_async_copy(nodes_hbm, nodes, in_s.at[0])
    load_coeffs = pltpu.make_async_copy(coeffs_hbm, coeffs, in_s.at[1])
    load_nodes.start()
    load_coeffs.start()

    barrier = pltpu.get_barrier_semaphore()
    for n in range(1, SLABS):
        tell(barrier, t, lax.rem(s + n, SLABS))
    for n in range(1, BLOCK):
        tell(barrier, base + lax.rem(place + n, BLOCK), s)

    cross_up = (place == BLOCK - 1) & (t < NT - 1)
    cross_down = (place == 0) & (t > 0)

    @pl.when(cross_up)
    def _():
        tell(barrier, t + 1, s)

    @pl.when(cross_down)
    def _():
        tell(barrier, t - 1, s)

    @pl.when(is_worker)
    def _():
        for n in range(1, NT // BLOCK):
            tell(barrier, lax.rem(t + BLOCK * n, NT), s)

    for dj in (-1, 0, 1):
        j = chunk + dj

        @pl.when(is_worker & (block > 0) & (j >= 0) & (j < SLABS))
        def _(j=j):
            for z in (0, 1):
                to, at = worker(z, j)
                tell(barrier, base - BLOCK + to, at)

    for buf in (ab, bb, cb):
        buf[:, 0:RIM, :] = jnp.zeros((DEPTH + 2, RIM, COLS), F32)
        buf[:, RIM + ROWS :, :] = jnp.zeros((DEPTH + 2, RIM, COLS), F32)

    @pl.when(s == 0)
    def _():
        for buf in (ab, bb, cb):
            buf[0, RIM : RIM + ROWS, :] = jnp.zeros((ROWS, COLS), F32)

    @pl.when(s == SLABS - 1)
    def _():
        for buf in (ab, bb, cb):
            buf[DEPTH + 1, RIM : RIM + ROWS, :] = jnp.zeros((ROWS, COLS), F32)

    kcp[:, 0:RIM, :] = jnp.zeros((7, RIM, LANES), F32)
    kcp[:, RIM + HALF :, :] = jnp.zeros((7, RIM, LANES), F32)
    rp[:, 0:RIM, :] = jnp.zeros((DEPTH, RIM, LANES), F32)
    rp[:, RIM + HALF :, :] = jnp.zeros((DEPTH, RIM, LANES), F32)

    def combine_a(p, i):
        here = pl.ds(pl.multiple_of(i * STRIP, STRIP), STRIP)
        there = pl.ds(pl.multiple_of(RIM + i * STRIP, 8), STRIP)
        ab[p + 1, there, :] = A0 * nodes[0, 0, p, here, :] + A1 * nodes[0, 1, p, here, :] + A2 * nodes[0, 2, p, here, :]

    load_nodes.wait()
    loop(strips, lambda i: combine_a(0, i))
    loop(strips, lambda i: combine_a(3, i))
    load_coeffs.wait()

    expect = 14 + jnp.where(cross_up, 1, 0) + jnp.where(cross_down, 1, 0)
    hands = 6 - jnp.where(chunk == 0, 2, 0) - jnp.where(chunk == SLABS - 1, 2, 0)
    expect = expect + jnp.where(is_worker, last_block, 0) + jnp.where(is_worker & (block < last_block), hands, 0)
    pl.semaphore_wait(barrier, expect)

    def halo(buf, phase, bounds, i, upward):
        rows = pl.ds(RIM + bounds[i], bounds[i + 1] - bounds[i])
        return pltpu.make_async_remote_copy(
            src_ref=buf.at[DEPTH if upward else 1, rows],
            dst_ref=buf.at[0 if upward else DEPTH + 1, rows],
            send_sem=halo_s.at[phase, int(upward), i],
            recv_sem=halo_r.at[phase, int(upward), i],
            device_id=(t, s + 1 if upward else s - 1),
            device_id_type=MESH,
        )

    def send_halo(buf, phase, bounds, i, upward):
        @pl.when(s < SLABS - 1 if upward else s > 0)
        def _():
            halo(buf, phase, bounds, i, upward).start()

    def take_halo(buf, phase, bounds, i, upward):
        @pl.when(s > 0 if upward else s < SLABS - 1)
        def _():
            halo(buf, phase, bounds, i, upward).wait_recv()

    for i in range(PIECES):
        send_halo(ab, 0, FIRST, i, False)
        send_halo(ab, 0, FIRST, i, True)
    for n in range(1, BLOCK):
        tell(known, base + lax.rem(place + n, BLOCK), s)

    narrow[...] = pair_matrix((COLS, LANES), 0, 0.25)
    wide[...] = pair_matrix((LANES, COLS), 1, 1.0)

    def restrict(p, across):
        pairs[p] = across
        return pairs[p, pl.ds(0, HALF, stride=2), :] + pairs[p, pl.ds(1, HALF, stride=2), :]

    def average(p, value):
        return restrict(p, times(value, narrow[...]))

    def prolong(p, value):
        pairs[p, pl.ds(0, HALF, stride=2), :] = value
        pairs[p, pl.ds(1, HALF, stride=2), :] = value
        return times(pairs[p], wide[...])

    def shift(src, dst, n, tm):
        return pltpu.make_async_remote_copy(
            src_ref=src, dst_ref=dst, send_sem=shift_s.at[n], recv_sem=shift_r.at[n],
            device_id=(tm, s), device_id_type=MESH,
        )

    send_w0 = shift(w0, wn, 0, t - 1)
    send_v2 = shift(v2, v2p, 1, t + 1)

    for p in range(DEPTH):
        w0[p] = average(p, nodes[0, 0, p])

    @pl.when(t > 0)
    def _():
        send_w0.start()

    @pl.when(t == NT - 1)
    def _():
        wn[...] = jnp.zeros_like(wn)

    def weights(p, i):
        here = pl.ds(pl.multiple_of(i * STRIP, STRIP), STRIP)
        k = [coeffs[m, p, here, :].astype(F32) for m in range(7)]
        for m in range(3):
            kf[m, p, here, :] = k[m]
            kf[3 + m, p, here, :] = 0.5 * k[3 + m]
        kf[6, p, here, :] = -(2.0 * (k[0] + k[1] + k[2]) + k[6])

    loop(DEPTH * strips, lambda n: weights(lax.div(n, strips), lax.rem(n, strips)))
    loop(strips, lambda i: combine_a(1, i))
    loop(strips, lambda i: combine_a(2, i))

    def force(buf, p, low, rows):
        window = slice(low, low + rows + 2 * RIM)
        here = slice(low, low + rows)
        return stencil(
            buf[p, window, :], buf[p + 1, window, :], buf[p + 2, window, :],
            [kf[m, p, here, :] for m in range(7)], rows + 2 * RIM, COLS, RIM, rows,
        )

    def first_node(p, low, rows):
        here = slice(low, low + rows)
        value = nodes[0, 0, p, here, :] + force(ab, p, low, rows)
        v1[p, here, :] = value
        bb[p + 1, RIM + low : RIM + low + rows, :] = (
            0.1 * value + B0 * nodes[0, 0, p, here, :] + (B1 - 0.1) * nodes[0, 1, p, here, :] + B2 * nodes[0, 2, p, here, :]
        )

    def last_node(p, low, rows):
        here = slice(low, low + rows)
        first = v1[p, here, :]
        value = first + force(bb, p, low, rows)
        v2[p, here, :] = value
        cb[p + 1, RIM + low : RIM + low + rows, :] = C0 * (nodes[0, 0, p, here, :] + value) + C1 * first

    def add_force(p, low, rows):
        here = slice(low, low + rows)
        out[0, 0, p, here, :] = nodes[0, 0, p, here, :] + force(cb, p, low, rows)

    def piece(fn, p, bounds, i):
        if bounds[i + 1] > bounds[i]:
            fn(p, bounds[i], bounds[i + 1] - bounds[i])

    inside = slice(RIM, RIM + HALF)
    k = []
    for m in range(7):
        across = jnp.dot(coeffs[m, block], narrow[...], preferred_element_type=F32)
        k.append(restrict(m % DEPTH, across))
    kcp[0, inside, :] = 0.2 * k[0]
    for m in range(1, 5):
        kcp[m, inside, :] = 0.05 * k[m]
    kcp[5, inside, :] = 0.025 * k[5]
    kcp[6, inside, :] = 1.0 - (0.4 * k[0] + 0.1 * (k[1] + k[2]) + 0.2 * k[6])
    for p in (1, 2):
        for i in range(PIECES):
            piece(first_node, p, FIRST, i)
    pl.semaphore_wait(known, BLOCK - 1)

    window = pl.ds(pl.multiple_of(8 * place, 8), WIN)

    def send_k(z):
        to, at = worker(z, place)
        src, dst = kcp.at[:, window], kb.at[:, s - 2 * z, block]
        own = (to == place) & (at == s)
        needed = s >= 2 if z else s <= 5
        copy = pltpu.make_async_remote_copy(
            src_ref=src, dst_ref=dst, send_sem=k_s.at[z], recv_sem=k_r.at[0],
            device_id=(base + to, at), device_id_type=MESH,
        )
        return needed & own, needed & jnp.logical_not(own), copy, pltpu.make_async_copy(src, dst, k_r.at[0])

    def start(parts):
        own, other, copy, local = parts

        @pl.when(own)
        def _():
            local.start()

        @pl.when(other)
        def _():
            copy.start()

    def end(parts):
        @pl.when(parts[1])
        def _():
            parts[2].wait_send()

    for z in (0, 1):
        start(send_k(z))

    def pass_k(n):
        part = kb.at[:, :, block]
        return pltpu.make_async_remote_copy(
            src_ref=part, dst_ref=part, send_sem=kf_s.at[n - 1], recv_sem=kf_r.at[block],
            device_id=(lax.rem(t + BLOCK * n, NT), s), device_id_type=MESH,
        )

    for i in range(PIECES):
        take_halo(ab, 0, FIRST, i, True)
        piece(first_node, 0, SECOND, i)
        send_halo(bb, 1, SECOND, i, False)
        take_halo(ab, 0, FIRST, i, False)
        piece(first_node, 3, SECOND, i)
        send_halo(bb, 1, SECOND, i, True)
        piece(last_node, 1, THIRD, i)
        piece(last_node, 2, THIRD, i)
    for i in range(PIECES):
        take_halo(bb, 1, SECOND, i, True)
        piece(last_node, 0, THIRD, i)
        send_halo(cb, 2, THIRD, i, False)
        take_halo(bb, 1, SECOND, i, False)
        piece(last_node, 3, THIRD, i)
        send_halo(cb, 2, THIRD, i, True)
        piece(add_force, 1, FOURTH, i)
        piece(add_force, 2, FOURTH, i)

    @pl.when(is_worker)
    def _():
        part = kb.at[:, :, block]
        pltpu.make_async_copy(part, part, k_r.at[0]).wait()
        for n in range(1, NT // BLOCK):

            @pl.when(block == NT // BLOCK - n)
            def _(n=n):
                pass_k(n).start()

    on_chip = lax.rem(place, 2) == 0

    @pl.when(on_chip)
    def _():
        send_v2.start()

    @pl.when(t < NT - 1)
    def _():
        send_w0.wait_recv()

    def right_side(p, low, rows):
        half_rows = rows // 2
        pairs[p, 0:rows] = times(out[0, 0, p, low : low + rows, :], narrow[...])
        both = pairs[p, pl.ds(0, half_rows, stride=2), :] + pairs[p, pl.ds(1, half_rows, stride=2), :]
        here = slice(low // 2, low // 2 + half_rows)
        rp[p, RIM + low // 2 : RIM + low // 2 + half_rows, :] = both - wn[p, here, :]

    def send_r(z, j):
        to, at = worker(z, j)
        src = rp.at[:, pl.ds(8 * j if isinstance(j, int) else pl.multiple_of(8 * j, 8), WIN)]
        dst = rb.at[place, pl.ds(DEPTH * s - 8 * z, DEPTH)]
        own = (to == place) & (at == s)
        needed = DEPTH * s + 3 >= 9 + place if z else DEPTH * s < 23 - place
        copy = pltpu.make_async_remote_copy(
            src_ref=src, dst_ref=dst, send_sem=r_s.at[z, j], recv_sem=r_r.at[place, s],
            device_id=(base + to, at), device_id_type=MESH,
        )
        return needed & own, needed & jnp.logical_not(own), copy, pltpu.make_async_copy(src, dst, r_r.at[place, s])

    done = 0
    for i in range(PIECES):
        take_halo(cb, 2, THIRD, i, True)
        piece(add_force, 0, FOURTH, i)
        take_halo(cb, 2, THIRD, i, False)
        piece(add_force, 3, FOURTH, i)
        for p in range(DEPTH):
            piece(right_side, p, FOURTH, i)
        ready = SLABS if i == PIECES - 1 else max(FOURTH[i + 1] // 16 - 1, 0)
        if ready > done:
            for z in (0, 1):
                for j in range(done, ready):
                    start(send_r(z, j))
        done = ready

    @pl.when(is_worker)
    def _():
        for n in range(1, NT // BLOCK):

            @pl.when(block != NT // BLOCK - n)
            def _(n=n):
                pass_k(n).start()

    @pl.when(jnp.logical_not(on_chip))
    def _():
        for z in (0, 1):
            loop(SLABS, lambda j, z=z: end(send_r(z, j)))

        @pl.when(t < NT - 1)
        def _():
            send_v2.start()

    def early_start():
        @pl.when(t > 0)
        def _():
            send_v2.wait_recv()
            for p in range(DEPTH):
                out[0, 0, p] = v2p[p] + prolong(p, average(p, nodes[0, 0, p] - v2p[p]))

        @pl.when(t == 0)
        def _():
            out[0, 0] = nodes[0, 0]

    for p in range(DEPTH):
        gap = prolong(p, wn[p] - average(p, v2[p]))
        out[0, 1, p] = v1[p] + 0.5 * gap
        out[0, 2, p] = v2[p] + gap

    pl.when(jnp.logical_not(is_worker))(early_start)

    def hand(z, dj):
        count = 8 if z else 16
        source = 9 if z else 1 + 8 * half
        target = jnp.where(half == 0, 1, 17) if z else source
        to, at = worker(1 - half if z else half, chunk + dj)
        return pltpu.make_async_remote_copy(
            src_ref=hb.at[BLOCK, pl.ds(source, count), pl.ds(8, 8)],
            dst_ref=hb.at[0, pl.ds(target, count), pl.ds(8 - 8 * dj, 8)],
            send_sem=hand_s.at[z, dj + 1],
            recv_sem=hand_r.at[z, dj + 1],
            device_id=(base + BLOCK + to, at),
            device_id_type=MESH,
        )

    def spread(h, n):
        to = 4 * half + n
        src = hb.at[h + 1, pl.ds(1 + 8 * half + DEPTH * n, DEPTH), pl.ds(8, 8)]
        dst = en.at[:, pl.ds(pl.multiple_of(8 * chunk, 8), 8)]
        own = (h == place) & (to == s)
        copy = pltpu.make_async_remote_copy(
            src_ref=src, dst_ref=dst, send_sem=e_s.at[h, n], recv_sem=e_r.at[0],
            device_id=(base + h, to), device_id_type=MESH,
        )
        return own, jnp.logical_not(own), copy, pltpu.make_async_copy(src, dst, e_r.at[0])

    def start_spread(h):
        for n in range(SLABS // 2):
            start(spread(h, n))

    @pl.when(is_worker)
    def _():
        def clear(h):
            hb[h, 0] = jnp.zeros((WIN, LANES), F32)
            hb[h, DEEP + 1] = jnp.zeros((WIN, LANES), F32)

        loop(BLOCK + 1, clear)

        @pl.when((block > 0) & (chunk == 0))
        def _():
            hb[0, 1 : DEEP + 1, 0:8, :] = jnp.zeros((DEEP, 8, LANES), F32)

        @pl.when((block > 0) & (chunk == SLABS - 1))
        def _():
            hb[0, 1 : DEEP + 1, 16:24, :] = jnp.zeros((DEEP, 8, LANES), F32)

        for n in range(1, NT // BLOCK):
            other = lax.rem(block + n, NT // BLOCK)
            part = kb.at[:, :, other]
            pltpu.make_async_copy(part, part, kf_r.at[other]).wait()
        for dj in (-1, 0, 1):
            @pl.when((block > 0) & (chunk - dj >= 0) & (chunk - dj < SLABS))
            def _(dj=dj):
                hand(0, dj).wait_recv()
                hand(1, dj).wait_recv()

        lane = lax.broadcasted_iota(jnp.int32, (WIN, LANES), 1)
        first, last = lane == 0, lane == LANES - 1

        def slopes(v):
            right, left = neighbours(v, 1, LANES, first, last)
            down, up = rows_around(v, WIN)
            over_y = right - left
            s_down, s_up = rows_around(over_y, WIN)
            return v, over_y, down - up, right + left, down + up, s_down - s_up

        def advance(h):
            count = lax.div(26 - h, 4)
            slab0 = half * (SLABS - count)
            quad = slab0 - 2 * half
            start_plane = DEPTH * quad

            def arrived(i):
                part = rb.at[h, pl.ds(start_plane + DEPTH * i, DEPTH)]
                pltpu.make_async_copy(part, part, r_r.at[h, slab0 + i]).wait()

            loop(count, arrived)

            def below():
                return slopes(hb[h, start_plane])[:3]


            def group(i, carry, planes):
                rows = slice(8, 16) if planes == 4 * DEPTH else slice(0, WIN)
                (low, low_y, low_x), here = carry
                for n in range(planes):
                    p = start_plane + DEPTH * i + n
                    above = slopes(hb[h, p + 2])
                    v, v_y, v_x, around_y, around_x, v_xy = here
                    k = [kb[m, quad + i + n // DEPTH, n % DEPTH, rows, :] for m in range(7)]
                    cut = lambda a: a[rows]
                    total = rb[h, p, rows, :] + k[0] * cut(above[0] + low) + k[1] * cut(around_x) + k[2] * cut(around_y)
                    total = total + k[3] * cut(above[2] - low_x) + k[4] * cut(above[1] - low_y)
                    hb[h + 1, p + 1, rows, :] = total + k[5] * cut(v_xy) + k[6] * cut(v)
                    low, low_y, low_x = v, v_y, v_x
                    here = above
                return (low, low_y, low_x), here

            since = jnp.where(block == 0, 1, 0)

            @pl.when(h < since)
            def _():
                hb[1, 1 : DEEP + 1] = rb[0]

            for some in (6, 5, 4):

                @pl.when((count == some) & (h >= since))
                def _(some=some):
                    group(0, (below(), slopes(hb[h, start_plane + 1])), DEPTH * some)

            @pl.when(block == last_block)
            def _():
                start_spread(h)

        loop(BLOCK, advance)

        @pl.when(block < last_block)
        def _():
            for z, dj in ((1, -1), (1, 1), (0, -1), (0, 1), (1, 0), (0, 0)):
                j = chunk + dj

                @pl.when((j >= 0) & (j < SLABS))
                def _(z=z, dj=dj):
                    hand(z, dj).start()

            loop(BLOCK, start_spread)

    pltpu.make_async_copy(en, en, e_r.at[0]).wait()
    forward = pltpu.make_async_remote_copy(
        src_ref=en, dst_ref=ec, send_sem=f_s.at[0], recv_sem=f_r.at[0], device_id=(t + 1, s), device_id_type=MESH
    )

    @pl.when(t < NT - 1)
    def _():
        forward.start()

    for p in range(DEPTH):
        gain = prolong(p, en[p])
        out[0, 2, p] += gain
        out[0, 1, p] += 0.5 * gain

    pl.when(is_worker)(early_start)

    @pl.when(t > 0)
    def _():
        forward.wait_recv()

        for p in range(DEPTH):
            gain = prolong(p, ec[p])
            out[0, 0, p] += gain
            out[0, 1, p] += 0.5 * gain

    for phase, (buf, bounds) in enumerate(((ab, FIRST), (bb, SECOND), (cb, THIRD))):
        for i in range(PIECES):

            @pl.when(s < SLABS - 1)
            def _(phase=phase, buf=buf, bounds=bounds, i=i):
                halo(buf, phase, bounds, i, True).wait_send()

            @pl.when(s > 0)
            def _(phase=phase, buf=buf, bounds=bounds, i=i):
                halo(buf, phase, bounds, i, False).wait_send()

    @pl.when(t > 0)
    def _():
        send_w0.wait_send()

    @pl.when(t < NT - 1)
    def _():
        send_v2.wait_send()
        forward.wait_send()

    for z in (0, 1):
        end(send_k(z))

        @pl.when(on_chip)
        def _(z=z):
            loop(SLABS, lambda j: end(send_r(z, j)))

    @pl.when(is_worker)
    def _():
        for n in range(1, NT // BLOCK):
            pass_k(n).wait_send()

        for dj in (-1, 0, 1):
            j = chunk + dj

            @pl.when((block < last_block) & (j >= 0) & (j < SLABS))
            def _(dj=dj):
                hand(0, dj).wait_send()
                hand(1, dj).wait_send()

        def end_spread(h):
            loop(4, lambda n: end(spread(h, n)))

        loop(BLOCK, end_spread)


def body(nodes, coefficients):
    dma = pltpu.SemaphoreType.DMA
    fine = (DEPTH, ROWS, COLS)
    rimmed = (DEPTH + 2, ROWS + 2 * RIM, COLS)
    coarse = (DEPTH, HALF, LANES)
    scratch = [
        (7,) + fine, rimmed, rimmed, rimmed, fine, fine, fine,
        (7, HALF + 2 * RIM, LANES), (DEPTH, HALF + 2 * RIM, LANES), coarse, coarse,
        (7, DEEP // DEPTH, DEPTH, WIN, LANES), (BLOCK, DEEP, WIN, LANES), (BLOCK + 1, DEEP + 2, WIN, LANES), coarse, coarse,
        (DEPTH, ROWS, LANES),
    ]
    sems = [(3, 2, PIECES), (3, 2, PIECES), (2,), (2,), (2,), (1,), (2, 8), (8, 8), (2, 3), (2, 3), (8, 4), (1,), (1,), (1,), (2,), (3,), (4,)]
    return pl.pallas_call(
        kernel,
        out_shape=jax.ShapeDtypeStruct(nodes.shape, F32),
        in_specs=[pl.BlockSpec(memory_space=pltpu.HBM)] * 2,
        out_specs=pl.BlockSpec(memory_space=pltpu.VMEM),
        scratch_shapes=[pltpu.VMEM(nodes.shape, F32), pltpu.VMEM(coefficients.shape, jnp.bfloat16)]
        + [pltpu.VMEM(shape, F32) for shape in scratch]
        + [pltpu.VMEM((LANES, COLS), jnp.bfloat16), pltpu.VMEM((COLS, LANES), jnp.bfloat16)]
        + [dma(shape) for shape in sems]
        + [pltpu.SemaphoreType.REGULAR],
        compiler_params=pltpu.CompilerParams(
            collective_id=0, has_side_effects=True, vmem_limit_bytes=48 * 1024 * 1024
        ),
        name="pfasst",
    )(nodes, coefficients)


def solution(mesh):
    return jax.shard_map(
        body,
        mesh=mesh,
        in_specs=(P("tm", None, "space", None, None), P(None, "space", None, None)),
        out_specs=P("tm", None, "space", None, None),
        check_vma=False,
    )
```
